256 devices in a mesh: gz: 8 (over y, core), xy: 32 (over z, x).
Axes of the slice: x: 4, y: 4, z: 8, core: 2. Of those that a mesh axis runs over, the one named last changes fastest.
Arguments:
- features: bfloat16 [2, 64, 128, 128, 128], P(None, None, 'gz', 'xy'), may hold values from -6 to 6
- cotangent: bfloat16 [2, 64, 128, 128, 128], P(None, None, 'gz', 'xy'), may hold values from -1.5 to 1.5
- spectral: bfloat16 [32, 32, 32, 64, 128], P('xy', 'gz'), may hold values from -0.75 to 0.75
- pointwise: bfloat16 [64, 64], replicated, may hold values from -0.75 to 0.75
- channel_bias: float32 [64], replicated, may hold values from -3 to 3
Outputs:
- layer_out: bfloat16 [2, 64, 128, 128, 128], P(None, None, 'gz', 'xy')
- input_grad: bfloat16 [2, 64, 128, 128, 128], P(None, None, 'gz', 'xy')
- spectral_grad: bfloat16 [32, 32, 32, 64, 128], P('xy', 'gz')
The draws below stay inside these ranges and needn't reach their ends.
All inputs are finite; a program needn't handle non-finite values.
Results may differ from the reference program's by a relative error of at most 0.025.
Values may be sent and summed in bfloat16 or wider, within the bound.
No kernel may reach another device: no remote copies, remote signals or barrier semaphores. Data moves between devices by JAX's collectives and lax.ppermute only.
A program may use at most 128 MiB of HBM per device.

```python
import math
import jax
import jax.numpy as jnp
from jax import lax

C = 64
NX = 128
NY = 128
NZ = 128
MX = 32
MY = 32
MZ = 32
B = 2


def levels(stream_key, shape, cuts, smallest, high):
    gain = 1.0
    for position, blocks in cuts:
        steps = jax.random.uniform(jax.random.fold_in(jax.random.fold_in(stream_key, 6), position), (blocks,), jnp.float32, smallest / len(cuts), high / len(cuts))
        gain = gain * jnp.repeat(jnp.exp(steps), shape[position] // blocks).reshape((-1,) + (1,) * (len(shape) - 1 - position))
    return gain


def bell_draw(key, extent, scale, limit, pieces=(), held_as=jnp.bfloat16):
    array = jax.random.normal(key, extent, jnp.float32) * scale
    if len(pieces) > 0:
        array = levels(key, extent, pieces, -0.22, 0.18) * array
    return jnp.clip(array, min=-limit, max=limit).astype(held_as)


def setup_inputs(seed: int = 0) -> dict:
    seeds = jax.random.split(jax.random.key(seed), 6)
    features = bell_draw(seeds[0], (B, C, NZ, NX, NY), 1.0, 6.0, ((2, 8), (3, 32)))
    cotangent = bell_draw(seeds[1], (B, C, NZ, NX, NY), 0.25, 1.5, ((2, 8), (3, 32)))
    spectral = bell_draw(seeds[2], (MY, MX, MZ, C, 2 * C), C ** -0.5, 0.75, ((0, 32), (1, 8)))
    pointwise = bell_draw(seeds[3], (C, C), C ** -0.5, 0.75)
    channel_bias = bell_draw(seeds[4], (C,), 0.5, 3.0, (), jnp.float32)
    return dict(features=features, cotangent=cotangent, spectral=spectral, pointwise=pointwise, channel_bias=channel_bias)


def rounded_table(values):
    return lax.optimization_barrier(values.astype(jnp.bfloat16)).astype(jnp.float32)


def frequency_list(total_modes, length, folded):
    counter = jnp.arange(total_modes, dtype=jnp.int32)
    if folded:
        return jnp.where(counter < total_modes // 2, counter, length - total_modes + counter)
    return counter


def twiddle(positions, frequency, length, orient):
    phases = (positions[:, None] * frequency[None, :]) % length
    angles = phases.astype(jnp.float32) * (2.0 * math.pi / length)
    cosine = rounded_table(jnp.cos(angles))
    sines = rounded_table(jnp.sin(angles))
    from_real = jnp.stack([cosine, orient * sines])
    from_imaginary = jnp.stack([-orient * sines, cosine])
    return jnp.stack([from_real, from_imaginary])


def axis_tables(orient):
    inner_table = twiddle(jnp.arange(NY, dtype=jnp.int32), frequency_list(MY, NY, False), NY, orient)
    pencil_table = twiddle(jnp.arange(NX, dtype=jnp.int32), frequency_list(MX, NX, True), NX, orient)
    slab_table = twiddle(jnp.arange(NZ, dtype=jnp.int32), frequency_list(MZ, NZ, True), NZ, orient)
    return inner_table, pencil_table, slab_table


def to_modes(grid_field, weights_inner, factor):
    inner_table, pencil_table, slab_table = axis_tables(-1.0)
    highest = lax.Precision.HIGHEST
    first_section = jnp.einsum('bczxy,syk->skbczx', grid_field.astype(jnp.float32), inner_table[0], precision=highest)
    first_section = (first_section * (factor * weights_inner)[None, :, None, None, None, None]).astype(jnp.bfloat16)
    middle = jnp.einsum('rkbczx,rsxj->skjbcz', first_section.astype(jnp.float32), pencil_table, precision=highest)
    return jnp.einsum('rkjbcz,rszm->skjmbc', middle, slab_table, precision=highest).astype(jnp.bfloat16)


def to_grid(spectrum, weights_inner, factor):
    inner_table, pencil_table, slab_table = axis_tables(1.0)
    highest = lax.Precision.HIGHEST
    middle = jnp.einsum('rkjmbc,rszm->skjbcz', spectrum.astype(jnp.float32), slab_table, precision=highest)
    partial_grid = jnp.einsum('rkjbcz,rsxj->skbczx', middle, pencil_table, precision=highest).astype(jnp.bfloat16)
    inner_back = inner_table[:, 0] * weights_inner[None, None, :]
    return jnp.einsum('skbczx,syk->bczxy', partial_grid.astype(jnp.float32), inner_back, precision=highest) * factor


def mix_modes(spectra, spectral):
    products = jnp.einsum('rkjmbi,kjmio->rkjmbo', spectra.astype(jnp.float32), spectral.astype(jnp.float32), precision=lax.Precision.HIGHEST)
    channels = spectral.shape[3]
    real_part = products[0, ..., :channels] - products[1, ..., channels:]
    imaginary = products[0, ..., channels:] + products[1, ..., :channels]
    return jnp.stack([real_part, imaginary]).astype(jnp.bfloat16)


def pair_grads(mode_grad):
    real_part = mode_grad[0]
    imaginary = mode_grad[1]
    return jnp.stack([jnp.concatenate([real_part, imaginary], axis=-1), jnp.concatenate([imaginary, -real_part], axis=-1)])


def gelu_parts(preact):
    argument = 0.7978845608 * (preact + 0.044715 * preact * preact * preact)
    squashed = jnp.tanh(argument)
    activated = 0.5 * preact * (1.0 + squashed)
    slopes = 0.5 * (1.0 + squashed) + 0.5 * preact * (1.0 - squashed * squashed) * 0.7978845608 * (1.0 + 3.0 * 0.044715 * preact * preact)
    return activated, slopes


def reference(features, cotangent, spectral, pointwise, channel_bias):
    highest = lax.Precision.HIGHEST
    forward_factor = (NX * NY * NZ) ** -0.5
    inverse_factor = 0.5 * (MX * MY * MZ) ** -0.5
    counter = jnp.arange(MY, dtype=jnp.int32)
    unit_weights = jnp.ones((MY,), jnp.float32)
    doubled = jnp.where(counter == 0, 1.0, 2.0).astype(jnp.float32)
    spectra = to_modes(features, unit_weights, forward_factor)
    mixed_modes = mix_modes(spectra, spectral)
    spatial = to_grid(mixed_modes, doubled, inverse_factor)
    local_term = jnp.einsum('bizxy,io->bozxy', features.astype(jnp.float32), pointwise.astype(jnp.float32), precision=highest)
    preact = spatial + local_term + channel_bias[None, :, None, None, None]
    activated, slopes = gelu_parts(preact)
    layer_out = activated.astype(jnp.bfloat16)
    pre_grad = (cotangent.astype(jnp.float32) * slopes).astype(jnp.bfloat16)
    mode_grad = to_modes(pre_grad, doubled, inverse_factor)
    paired = pair_grads(mode_grad).astype(jnp.float32)
    spectra_grad = jnp.einsum('rkjmbo,kjmio->rkjmbi', paired, spectral.astype(jnp.float32), precision=highest).astype(jnp.bfloat16)
    spectral_grad = jnp.einsum('rkjmbi,rkjmbo->kjmio', spectra.astype(jnp.float32), paired, precision=highest).astype(jnp.bfloat16)
    back_term = jnp.einsum('bozxy,io->bizxy', pre_grad.astype(jnp.float32), pointwise.astype(jnp.float32), precision=highest)
    input_grad = (to_grid(spectra_grad, unit_weights, forward_factor) + back_term).astype(jnp.bfloat16)
    return (layer_out, input_grad, spectral_grad)
```

```python
import functools
import math

import jax
import jax.numpy as jnp
import ml_dtypes
import numpy as np
from jax import lax
from jax.experimental import pallas as pl
from jax.experimental.pallas import tpu as pltpu
from jax.sharding import PartitionSpec as P

C = 64
NX = 128
NY = 128
NZ = 128
MX = 32
MY = 32
MZ = 32
BATCH = 2
GZ = 8
XY = 32
BC = BATCH * C
ZL = NZ // GZ
XL = NX // XY
ZP = 2
PAIRS = ZL // ZP
ROWS = ZP * 2 * XL
BF = jnp.bfloat16
F32 = jnp.float32
FORWARD = (NX * NY * NZ) ** (-0.5)
INVERSE = 0.5 * (MX * MY * MZ) ** (-0.5)


def rounded(values):
    return values.astype(np.float32).astype(ml_dtypes.bfloat16).astype(np.float32)


def cos_sin(length, modes, folded):
    freq = np.arange(modes)
    if folded:
        freq = np.where(freq < modes // 2, freq, length - modes + freq)
    phase = (np.arange(length)[:, None] * freq[None, :]) % length
    angle = phase.astype(np.float32) * np.float32(2.0 * math.pi / length)
    return rounded(np.cos(angle)), rounded(np.sin(angle))


@functools.lru_cache(maxsize=None)
def tables():
    cy, sy = cos_sin(NY, MY, False)
    cx, sx = cos_sin(NX, MX, True)
    cz, sz = cos_sin(NZ, MZ, True)
    same = np.eye(ZP * XL, dtype=np.float32).reshape(ZP, XL, ZP, XL)
    part = np.stack([cy, -sy])
    unit = np.einsum("ryk,zxwv->kzrxwvy", part, same).reshape(MY * ROWS, ZP * XL * NY)
    scale = np.where(np.arange(MY) == 0, 1.0, 2.0).astype(np.float32)
    doubled = unit * np.repeat(scale, ROWS)[:, None]
    z2 = np.eye(ZP, dtype=np.float32)
    fx = np.stack([np.stack([cx, sx]), np.stack([-sx, cx])])
    fx = fx.reshape(2, 2, XY, XL, MX)
    x_fwd = np.einsum("sopvk,zw->kszpwov", fx, z2).reshape(MX * 2 * ZP, XY * ROWS)
    gx = np.stack([np.stack([cx, -sx]), np.stack([sx, cx])])
    gx = gx.reshape(2, 2, XY, XL, MX)
    x_inv = np.einsum("sopvk,zw->pzsvkow", gx, z2).reshape(XY * ROWS, MX * 2 * ZP)
    kx = MX // GZ
    kxe = np.eye(kx, dtype=np.float32)
    fz = np.stack([np.stack([cz, sz]), np.stack([-sz, cz])])
    fz = fz.reshape(2, 2, GZ, PAIRS, ZP, MZ)
    z_fwd = np.einsum("sogjzm,kl->skmgjloz", fz, kxe).reshape(2 * kx * MZ, GZ * PAIRS * kx * 2 * ZP)
    gz = np.stack([np.stack([cz, -sz]), np.stack([sz, cz])])
    gz = gz.reshape(2, 2, GZ, PAIRS, ZP, MZ)
    z_inv = np.einsum("sogjzm,kl->gjkszolm", gz, kxe).reshape(GZ * PAIRS * kx * 2 * ZP, 2 * kx * MZ)
    made = dict(
        unit=unit,
        doubled=doubled,
        doubled_t=doubled.T,
        x_fwd=x_fwd,
        x_inv=x_inv,
        z_fwd=z_fwd,
        z_inv=z_inv,
    )
    return {k: np.ascontiguousarray(v).astype(ml_dtypes.bfloat16) for k, v in made.items()}


def dot(a, b, dims=((1,), (0,))):
    return lax.dot_general(a, b, (dims, ((), ())), preferred_element_type=F32)


VM = 48 * 1024 * 1024


def call(kernel, outs, grid, in_specs, out_specs, scratch, name, flops, nbytes):
    return pl.pallas_call(
        kernel,
        out_shape=outs,
        grid=grid,
        in_specs=in_specs,
        out_specs=out_specs,
        scratch_shapes=scratch,
        name=name,
        compiler_params=pltpu.CompilerParams(vmem_limit_bytes=VM),
        cost_estimate=pl.CostEstimate(flops=flops, bytes_accessed=nbytes, transcendentals=0),
    )


STEPS = PAIRS // 2
CELLS = ZP * XL
STEP_CELLS = 2 * CELLS


def whole(shape):
    return pl.BlockSpec(shape, lambda i: (0,) * len(shape))


def first_kernel(x_ref, table_ref, out_ref, wide_ref):
    wide_ref[...] = x_ref[...].astype(F32).reshape(BC * STEP_CELLS, NY)
    rows = []
    for j in range(2):
        cells = [
            wide_ref[pl.ds(j * CELLS + t, BC, stride=STEP_CELLS), :].astype(BF)
            for t in range(CELLS)
        ]
        rows.append(jnp.concatenate(cells, axis=1))
    both = jnp.concatenate(rows, axis=0)
    modes = (dot(table_ref[...], both, ((1,), (1,))) * FORWARD).astype(BF)
    for j in range(2):
        out_ref[:, j * ROWS : (j + 1) * ROWS, :] = modes[:, j * BC : (j + 1) * BC].reshape(
            MY, ROWS, BC
        )


def y_first(x, table):
    return call(
        first_kernel,
        jax.ShapeDtypeStruct((MY, PAIRS * ROWS, BC), BF),
        (STEPS,),
        [
            pl.BlockSpec((BC, STEP_CELLS, NY), lambda i: (0, i, 0)),
            whole(table.shape),
        ],
        pl.BlockSpec((MY, 2 * ROWS, BC), lambda i: (0, i, 0)),
        [pltpu.VMEM((BC * STEP_CELLS, NY), F32)],
        "y_first",
        2 << 29,
        4 << 20,
    )(x, table)


def to_lanes_kernel(x_ref, out_ref, wide_ref):
    wide_ref[...] = x_ref[...].astype(F32).reshape(BC * STEP_CELLS, NY)
    for t in range(STEP_CELLS):
        cell = wide_ref[pl.ds(t, BC, stride=STEP_CELLS), :]
        out_ref[t * NY : (t + 1) * NY, :] = cell.T.astype(BF)


def to_lanes(x):
    return call(
        to_lanes_kernel,
        jax.ShapeDtypeStruct((ZL * XL * NY, BC), BF),
        (STEPS,),
        [pl.BlockSpec((BC, STEP_CELLS, NY), lambda i: (0, i, 0))],
        pl.BlockSpec((STEP_CELLS * NY, BC), lambda i: (i, 0)),
        [pltpu.VMEM((BC * STEP_CELLS, NY), F32)],
        "to_lanes",
        0,
        12 << 20,
    )(x)


def from_lanes_kernel(x_ref, out_ref, wide_ref):
    for t in range(STEP_CELLS):
        cell = x_ref[t * NY : (t + 1) * NY, :].astype(F32)
        wide_ref[pl.ds(t, BC, stride=STEP_CELLS), :] = cell.T
    out_ref[...] = wide_ref[...].reshape(BC, STEP_CELLS, NY).astype(BF)


def from_lanes(x):
    return call(
        from_lanes_kernel,
        jax.ShapeDtypeStruct((BC, ZL * XL, NY), BF),
        (STEPS,),
        [pl.BlockSpec((STEP_CELLS * NY, BC), lambda i: (i, 0))],
        pl.BlockSpec((BC, STEP_CELLS, NY), lambda i: (0, i, 0)),
        [pltpu.VMEM((BC * STEP_CELLS, NY), F32)],
        "from_lanes",
        0,
        12 << 20,
    )(x)


def x_forward_kernel(recv_ref, table_ref, out_ref):
    wide = jnp.concatenate(
        [
            recv_ref[:, j * ROWS : (j + 1) * ROWS, :].reshape(XY * ROWS, BC)
            for j in range(2)
        ],
        axis=1,
    )
    done = dot(table_ref[...], wide).astype(BF)
    for j in range(2):
        out_ref[:, j * ROWS : (j + 1) * ROWS, :] = done[:, j * BC : (j + 1) * BC].reshape(
            GZ, ROWS, BC
        )


def x_forward(recv, table):
    return call(
        x_forward_kernel,
        jax.ShapeDtypeStruct((GZ, PAIRS * ROWS, BC), BF),
        (STEPS,),
        [
            pl.BlockSpec((XY, 2 * ROWS, BC), lambda i: (0, i, 0)),
            whole(table.shape),
        ],
        pl.BlockSpec((GZ, 2 * ROWS, BC), lambda i: (0, i, 0)),
        [],
        "x_forward",
        1 << 27,
        2 << 20,
    )(recv, table)


def x_inverse_kernel(recv_ref, table_ref, out_ref):
    wide = jnp.concatenate(
        [
            recv_ref[:, j * ROWS : (j + 1) * ROWS, :].reshape(GZ * ROWS, BC)
            for j in range(2)
        ],
        axis=1,
    )
    done = dot(table_ref[...], wide).astype(BF)
    for j in range(2):
        out_ref[:, j * ROWS : (j + 1) * ROWS, :] = done[:, j * BC : (j + 1) * BC].reshape(
            XY, ROWS, BC
        )


def x_inverse(recv, table):
    return call(
        x_inverse_kernel,
        jax.ShapeDtypeStruct((XY, PAIRS * ROWS, BC), BF),
        (STEPS,),
        [
            pl.BlockSpec((GZ, 2 * ROWS, BC), lambda i: (0, i, 0)),
            whole(table.shape),
        ],
        pl.BlockSpec((XY, 2 * ROWS, BC), lambda i: (0, i, 0)),
        [],
        "x_inverse",
        1 << 27,
        2 << 20,
    )(recv, table)


PAIR_CELLS = CELLS * NY


def middle_kernel(
    recv_ref, x_ref, cot_ref, inv_ref, fwd_ref, mix_ref, bias_ref, send_ref, layer_ref, pre_ref, sum_ref, cat_ref
):
    wide = jnp.concatenate(
        [
            recv_ref[:, j * ROWS : (j + 1) * ROWS, :].reshape(MY * ROWS, BC)
            for j in range(2)
        ],
        axis=1,
    )
    sum_ref[...] = dot(inv_ref[...], wide)

    def chunk(step, _):
        at = pl.ds(pl.multiple_of(step * NY, NY), NY)
        for j in range(2):
            rows = pl.ds(pl.multiple_of(j * PAIR_CELLS + step * NY, NY), NY)
            local = dot(x_ref[rows, :], mix_ref[...])
            p = sum_ref[at, j * BC : (j + 1) * BC] * INVERSE + local + bias_ref[...]
            square = p * p
            inner = 0.7978845608 + (0.7978845608 * 0.044715) * square
            half = 0.5 + 0.5 * jnp.tanh(p * inner)
            layer_ref[rows, :] = (p * half).astype(BF)
            tail = (2.0 * 0.7978845608) + (6.0 * 0.7978845608 * 0.044715) * square
            slope = half + half * (1.0 - half) * (p * tail)
            grad = (cot_ref[rows, :].astype(F32) * slope).astype(BF)
            pre_ref[rows, :] = grad
            cat_ref[at, j * BC : (j + 1) * BC] = grad
        return 0

    lax.fori_loop(0, CELLS, chunk, 0)
    modes = (dot(fwd_ref[...], cat_ref[...]) * INVERSE).astype(BF)
    for j in range(2):
        send_ref[:, j * ROWS : (j + 1) * ROWS, :] = modes[:, j * BC : (j + 1) * BC].reshape(
            MY, ROWS, BC
        )


def middle(recv, x, cot, inv, fwd, mix, bias):
    flat = jax.ShapeDtypeStruct((ZL * XL * NY, BC), BF)
    step_rows = pl.BlockSpec((STEP_CELLS * NY, BC), lambda i: (i, 0))
    block = pl.BlockSpec((MY, 2 * ROWS, BC), lambda i: (0, i, 0))
    return call(
        middle_kernel,
        [jax.ShapeDtypeStruct((MY, PAIRS * ROWS, BC), BF), flat, flat],
        (STEPS,),
        [
            block,
            step_rows,
            step_rows,
            whole(inv.shape),
            whole(fwd.shape),
            whole(mix.shape),
            whole(bias.shape),
        ],
        [block, step_rows, step_rows],
        [
            pltpu.VMEM((PAIR_CELLS, 2 * BC), F32),
            pltpu.VMEM((PAIR_CELLS, 2 * BC), BF),
        ],
        "middle",
        4 << 29,
        12 << 20,
    )(recv, x, cot, inv, fwd, mix, bias)


def last_kernel(recv_ref, pre_ref, inv_ref, mix_ref, out_ref, wide_ref):
    for j in range(2):
        modes = recv_ref[:, j * ROWS : (j + 1) * ROWS, :].reshape(MY * ROWS, BC)
        cells = dot(modes, inv_ref[...], ((0,), (0,))) * FORWARD
        cells += dot(mix_ref[...], pre_ref[j * PAIR_CELLS : (j + 1) * PAIR_CELLS, :], ((1,), (1,)))
        for t in range(CELLS):
            wide_ref[pl.ds(j * CELLS + t, BC, stride=STEP_CELLS), :] = cells[:, t * NY : (t + 1) * NY]
    out_ref[...] = wide_ref[...].reshape(BC, STEP_CELLS, NY).astype(BF)


def last(recv, pre, inv, mix):
    return call(
        last_kernel,
        jax.ShapeDtypeStruct((BC, ZL * XL, NY), BF),
        (STEPS,),
        [
            pl.BlockSpec((MY, 2 * ROWS, BC), lambda i: (0, i, 0)),
            pl.BlockSpec((STEP_CELLS * NY, BC), lambda i: (i, 0)),
            whole(inv.shape),
            whole(mix.shape),
        ],
        pl.BlockSpec((BC, STEP_CELLS, NY), lambda i: (0, i, 0)),
        [pltpu.VMEM((BC * STEP_CELLS, NY), F32)],
        "last",
        4 << 29,
        8 << 20,
    )(recv, pre, inv, mix)


def exchange(x, axis):
    return lax.all_to_all(x, axis, split_axis=0, concat_axis=0, tiled=True)


KX = MX // GZ


def z_forward(recv, table):
    modes = dot(table, recv.reshape(GZ * PAIRS * ROWS, BC))
    return modes.astype(BF).reshape(2, KX, MZ, BATCH, C)


def z_inverse(modes, table):
    return dot(table, modes.reshape(2 * KX * MZ, BC)).astype(BF).reshape(GZ, PAIRS * ROWS, BC)


def body(features, cotangent, spectral, pointwise, channel_bias):
    t = {k: jnp.asarray(v) for k, v in tables().items()}
    x = features.reshape(BC, ZL * XL, NY)
    cot = cotangent.reshape(BC, ZL * XL, NY)
    weights = spectral[0]
    mix = jnp.zeros((BATCH, C, BATCH, C), BF)
    mix = mix.at[0, :, 0, :].set(pointwise).at[1, :, 1, :].set(pointwise).reshape(BC, BC)
    bias = jnp.tile(channel_bias, BATCH)[None, :]

    recv = exchange(y_first(x, t["unit"]), "xy")
    x_lanes = to_lanes(x)
    recv = exchange(x_forward(recv, t["x_fwd"]), "gz")
    spectra = z_forward(recv, t["z_fwd"])
    products = jnp.einsum("rkmbi,kmio->rkmbo", spectra, weights, preferred_element_type=F32)
    mixed = jnp.stack(
        [
            products[0, ..., :C] - products[1, ..., C:],
            products[0, ..., C:] + products[1, ..., :C],
        ]
    ).astype(BF)
    recv = exchange(z_inverse(mixed, t["z_inv"]), "gz")
    recv = exchange(x_inverse(recv, t["x_inv"]), "xy")
    cot_lanes = to_lanes(cot)
    send, layer, pre = middle(
        recv, x_lanes, cot_lanes, t["doubled_t"], t["doubled"], mix, bias
    )
    recv = exchange(send, "xy")
    layer_out = from_lanes(layer)
    recv = exchange(x_forward(recv, t["x_fwd"]), "gz")
    mode_grad = z_forward(recv, t["z_fwd"])
    real, imag = mode_grad[0], mode_grad[1]
    paired = jnp.stack(
        [
            jnp.concatenate([real, imag], axis=-1),
            jnp.concatenate([imag, -real], axis=-1),
        ]
    )
    spectra_grad = jnp.einsum(
        "rkmbo,kmio->rkmbi", paired, weights, preferred_element_type=F32
    ).astype(BF)
    recv = exchange(z_inverse(spectra_grad, t["z_inv"]), "gz")
    recv = exchange(x_inverse(recv, t["x_inv"]), "xy")
    spectral_grad = jnp.einsum(
        "rkmbi,rkmbo->kmio", spectra, paired, preferred_element_type=F32
    ).astype(BF)
    input_grad = last(recv, pre, t["unit"], mix)
    return (
        layer_out.reshape(features.shape),
        input_grad.reshape(features.shape),
        spectral_grad[None],
    )


def solution(mesh):
    field = P(None, None, "gz", "xy", None)
    modes = P("xy", "gz", None, None, None)
    return jax.shard_map(
        body,
        mesh=mesh,
        in_specs=(field, field, modes, P(), P()),
        out_specs=(field, field, modes),
        check_vma=False,
    )
```

```python
import functools
import math

import jax
import jax.numpy as jnp
import ml_dtypes
import numpy as np
from jax import lax
from jax.experimental import pallas as pl
from jax.experimental.pallas import tpu as pltpu
from jax.sharding import PartitionSpec as P

C = 64
NX = 128
NY = 128
NZ = 128
MX = 32
MY = 32
MZ = 32
BATCH = 2
GZ = 8
XY = 32
BC = BATCH * C
ZL = NZ // GZ
XL = NX // XY
ZP = 2
PAIRS = ZL // ZP
SUB = 2 * XL
ROWS = ZP * SUB
BF = jnp.bfloat16
F32 = jnp.float32
FORWARD = (NX * NY * NZ) ** (-0.5)
INVERSE = 0.5 * (MX * MY * MZ) ** (-0.5)


def rounded(values):
    return values.astype(np.float32).astype(ml_dtypes.bfloat16).astype(np.float32)


def cos_sin(length, modes, folded):
    freq = np.arange(modes)
    if folded:
        freq = np.where(freq < modes // 2, freq, length - modes + freq)
    phase = (np.arange(length)[:, None] * freq[None, :]) % length
    angle = phase.astype(np.float32) * np.float32(2.0 * math.pi / length)
    return rounded(np.cos(angle)), rounded(np.sin(angle))


@functools.lru_cache(maxsize=None)
def tables():
    cy, sy = cos_sin(NY, MY, False)
    cx, sx = cos_sin(NX, MX, True)
    cz, sz = cos_sin(NZ, MZ, True)
    same = np.eye(XL, dtype=np.float32)
    part = np.stack([cy, -sy])
    unit = np.einsum("ryk,xv->krxvy", part, same).reshape(MY * SUB, XL * NY)
    scale = np.where(np.arange(MY) == 0, 1.0, 2.0).astype(np.float32)
    doubled = unit * np.repeat(scale, SUB)[:, None]
    z2 = np.eye(ZP, dtype=np.float32)
    fx = np.stack([np.stack([cx, sx]), np.stack([-sx, cx])])
    fx = fx.reshape(2, 2, XY, XL, MX)
    x_fwd = np.einsum("sopvk,zw->kszpwov", fx, z2).reshape(MX * 2 * ZP, XY * ROWS)
    gx = np.stack([np.stack([cx, -sx]), np.stack([sx, cx])])
    gx = gx.reshape(2, 2, XY, XL, MX)
    x_inv = np.einsum("sopvk,zw->pzsvkow", gx, z2).reshape(XY * ROWS, MX * 2 * ZP)
    kx = MX // GZ
    kxe = np.eye(kx, dtype=np.float32)
    fz = np.stack([np.stack([cz, sz]), np.stack([-sz, cz])])
    fz = fz.reshape(2, 2, GZ, PAIRS, ZP, MZ)
    z_fwd = np.einsum("sogjzm,kl->skmgjloz", fz, kxe).reshape(2 * kx * MZ, GZ * PAIRS * kx * 2 * ZP)
    gz = np.stack([np.stack([cz, -sz]), np.stack([sz, cz])])
    gz = gz.reshape(2, 2, GZ, PAIRS, ZP, MZ)
    z_inv = np.einsum("sogjzm,kl->gjkszolm", gz, kxe).reshape(GZ * PAIRS * kx * 2 * ZP, 2 * kx * MZ)
    made = dict(
        unit=unit,
        doubled=doubled,
        doubled_t=doubled.T,
        x_fwd=x_fwd,
        x_inv=x_inv,
        z_fwd=z_fwd,
        z_inv=z_inv,
    )
    return {k: np.ascontiguousarray(v).astype(ml_dtypes.bfloat16) for k, v in made.items()}


def dot(a, b, dims=((1,), (0,))):
    return lax.dot_general(a, b, (dims, ((), ())), preferred_element_type=F32)


VM = 24 * 1024 * 1024
STEPS = PAIRS // 2
CELLS = ZP * XL
STEP_CELLS = 2 * CELLS
PLANE = XL * NY
VMEM = pl.BlockSpec(memory_space=pltpu.VMEM)
REMOTE = pl.BlockSpec(memory_space=pltpu.HBM)


def far(x):
    return pltpu.with_memory_space_constraint(x, pltpu.HBM)


def call(kernel, outs, in_specs, out_specs, scratch, name, flops, nbytes):
    return pl.pallas_call(
        kernel,
        out_shape=outs,
        in_specs=in_specs,
        out_specs=out_specs,
        scratch_shapes=scratch,
        name=name,
        compiler_params=pltpu.CompilerParams(vmem_limit_bytes=VM),
        cost_estimate=pl.CostEstimate(flops=flops, bytes_accessed=nbytes, transcendentals=0),
    )


def split_pair(block):
    wide = block.astype(F32)
    n = wide.shape[0]
    halves = [wide[:, z * SUB : (z + 1) * SUB, :].reshape(n * SUB, BC) for z in range(ZP)]
    return jnp.concatenate(halves, axis=1).astype(BF)


def join_pair(wide):
    n = wide.shape[0] // SUB
    halves = [wide[:, z * BC : (z + 1) * BC].reshape(n, SUB, BC) for z in range(ZP)]
    return jnp.concatenate(halves, axis=1).astype(BF)


def chunk_of(ref, step):
    return ref.at[:, step * STEP_CELLS : (step + 1) * STEP_CELLS, :]


def aligned(index, size):
    if isinstance(index, int):
        return index * size
    return pl.multiple_of(index * size, size)


def rows_of(ref, step):
    return ref.at[step * STEP_CELLS * NY : (step + 1) * STEP_CELLS * NY, :]


def first_kernel(x_ref, far_ref, out_ref, in_ref, table_ref, wide_ref, sem):
    copies = [
        pltpu.make_async_copy(chunk_of(x_ref, i), in_ref.at[i], sem.at[i]) for i in range(STEPS)
    ]
    fetch = pltpu.make_async_copy(far_ref, table_ref, sem.at[STEPS])
    copies[0].start()
    fetch.start()
    copies[1].start()
    for i in range(STEPS):
        copies[i].wait()
        if i + 2 < STEPS:
            copies[i + 2].start()
        if i == 0:
            fetch.wait()
        wide_ref[i % 2] = in_ref[i].astype(F32).reshape(BC * STEP_CELLS, NY)
        for j in range(2):
            planes = []
            for z in range(ZP):
                cells = [
                    wide_ref[i % 2, pl.ds(j * CELLS + z * XL + t, BC, stride=STEP_CELLS), :].astype(BF)
                    for t in range(XL)
                ]
                planes.append(jnp.concatenate(cells, axis=1))
            both = jnp.concatenate(planes, axis=0)
            modes = dot(table_ref[...], both, ((1,), (1,)))
            at = (2 * i + j) * ROWS
            out_ref[:, at : at + ROWS, :] = join_pair(modes)


def y_first(x, table):
    return call(
        first_kernel,
        jax.ShapeDtypeStruct((MY, PAIRS * ROWS, BC), BF),
        [REMOTE, REMOTE],
        VMEM,
        [
            pltpu.VMEM((STEPS, BC, STEP_CELLS, NY), BF),
            pltpu.VMEM(table.shape, BF),
            pltpu.VMEM((2, BC * STEP_CELLS, NY), F32),
            pltpu.SemaphoreType.DMA((STEPS + 1,)),
        ],
        "y_first",
        1 << 29,
        4 << 20,
    )(far(x), far(table))


def to_lanes_kernel(x_ref, out_ref, in_ref, made_ref, wide_ref, sem, out_sem):
    copies = [
        pltpu.make_async_copy(chunk_of(x_ref, i), in_ref.at[i], sem.at[i]) for i in range(STEPS)
    ]
    for copy in copies:
        copy.start()
    outs = []
    for i in range(STEPS):
        copies[i].wait()
        wide_ref[i % 2] = in_ref[i].astype(F32).reshape(BC * STEP_CELLS, NY)
        for t in range(STEP_CELLS):
            cell = wide_ref[i % 2, pl.ds(t, BC, stride=STEP_CELLS), :]
            made_ref[i, t * NY : (t + 1) * NY, :] = cell.T.astype(BF)
        outs.append(pltpu.make_async_copy(made_ref.at[i], rows_of(out_ref, i), out_sem.at[i]))
        outs[i].start()
    for copy in outs:
        copy.wait()


def to_lanes(x):
    return call(
        to_lanes_kernel,
        jax.ShapeDtypeStruct((ZL * XL * NY, BC), BF),
        [REMOTE],
        REMOTE,
        [
            pltpu.VMEM((STEPS, BC, STEP_CELLS, NY), BF),
            pltpu.VMEM((STEPS, STEP_CELLS * NY, BC), BF),
            pltpu.VMEM((2, BC * STEP_CELLS, NY), F32),
            pltpu.SemaphoreType.DMA((STEPS,)),
            pltpu.SemaphoreType.DMA((STEPS,)),
        ],
        "to_lanes",
        0,
        12 << 20,
    )(far(x))


def from_lanes_kernel(x_ref, out_ref, in_ref, made_ref, wide_ref, in_sem, sem):
    fetches = [
        pltpu.make_async_copy(rows_of(x_ref, i), in_ref.at[i], in_sem.at[i]) for i in range(STEPS)
    ]
    for copy in fetches:
        copy.start()
    copies = []
    for i in range(STEPS):
        fetches[i].wait()
        for t in range(STEP_CELLS):
            cell = in_ref[i, t * NY : (t + 1) * NY, :].astype(F32)
            wide_ref[i % 2, pl.ds(t, BC, stride=STEP_CELLS), :] = cell.T
        made_ref[i] = wide_ref[i % 2].reshape(BC, STEP_CELLS, NY).astype(BF)
        copies.append(pltpu.make_async_copy(made_ref.at[i], chunk_of(out_ref, i), sem.at[i]))
        copies[i].start()
    for copy in copies:
        copy.wait()


def from_lanes(x):
    return call(
        from_lanes_kernel,
        jax.ShapeDtypeStruct((BC, ZL * XL, NY), BF),
        [REMOTE],
        REMOTE,
        [
            pltpu.VMEM((STEPS, STEP_CELLS * NY, BC), BF),
            pltpu.VMEM((STEPS, BC, STEP_CELLS, NY), BF),
            pltpu.VMEM((2, BC * STEP_CELLS, NY), F32),
            pltpu.SemaphoreType.DMA((STEPS,)),
            pltpu.SemaphoreType.DMA((STEPS,)),
        ],
        "from_lanes",
        0,
        12 << 20,
    )(far(x))


def x_kernel(groups_in, groups_out, scale, recv_ref, table_ref, out_ref):
    for i in range(STEPS):
        wide = jnp.concatenate(
            [
                recv_ref[:, (2 * i + j) * ROWS : (2 * i + j + 1) * ROWS, :].reshape(
                    groups_in * ROWS, BC
                )
                for j in range(2)
            ],
            axis=1,
        )
        done = (dot(table_ref[...], wide) * scale).astype(BF)
        for j in range(2):
            at = (2 * i + j) * ROWS
            out_ref[:, at : at + ROWS, :] = done[:, j * BC : (j + 1) * BC].reshape(
                groups_out, ROWS, BC
            )


def x_transform(recv, table, groups_out, scale, name):
    return call(
        functools.partial(x_kernel, recv.shape[0], groups_out, scale),
        jax.ShapeDtypeStruct((groups_out, PAIRS * ROWS, BC), BF),
        [VMEM, VMEM],
        VMEM,
        [],
        name,
        1 << 27,
        2 << 20,
    )(recv, table)


def middle_kernel(
    recv_ref,
    x_far,
    cot_far,
    inv_far,
    fwd_far,
    mix_ref,
    bias_ref,
    send_ref,
    layer_ref,
    pre_ref,
    x_ref,
    cot_ref,
    inv_ref,
    fwd_ref,
    cat_ref,
    x_sem,
    cot_sem,
    table_sem,
):
    depth = ZP * PLANE

    def part(ref, pair):
        return ref.at[pl.ds(aligned(pair, depth), depth), :]

    def move(source, target, sem, pair):
        return pltpu.make_async_copy(part(source, pair), part(target, pair), sem.at[pair])

    tables = [
        pltpu.make_async_copy(inv_far, inv_ref, table_sem.at[0]),
        pltpu.make_async_copy(fwd_far, fwd_ref, table_sem.at[1]),
    ]

    def fetch(pair):
        move(x_far, x_ref, x_sem, pair).start()
        move(cot_far, cot_ref, cot_sem, pair).start()

    tables[0].start()
    fetch(0)
    tables[1].start()
    fetch(1)

    def forward(pair):
        modes = dot(fwd_ref[...], cat_ref[pair & 1])
        send_ref[:, pl.ds(aligned(pair, ROWS), ROWS), :] = join_pair(modes)

    mix = mix_ref[...]
    none = jnp.zeros_like(mix)
    lower = jnp.concatenate(
        [jnp.concatenate([mix, none], axis=1), jnp.concatenate([none, mix], axis=1)], axis=0
    )
    bias = bias_ref[...]

    tables[0].wait()

    def step(pair, first=False, final=False):
        if not final:
            fetch(pair + 2)
        if not first:
            forward(pair - 1)
        block = recv_ref[:, pl.ds(aligned(pair, ROWS), ROWS), :]
        right = jnp.concatenate([split_pair(block), lower], axis=0)
        base = aligned(pair, depth)
        move(x_far, x_ref, x_sem, pair).wait()
        move(cot_far, cot_ref, cot_sem, pair).wait()
        for t in range(XL):
            cells = [pl.ds(base + z * PLANE + t * NY, NY) for z in range(ZP)]
            left = jnp.concatenate(
                [inv_ref[t * NY : (t + 1) * NY, :]] + [x_ref[rows, :] for rows in cells], axis=1
            )
            total = dot(left, right)
            for z, rows in enumerate(cells):
                p = total[:, z * BC : (z + 1) * BC] + bias
                square = p * p
                inner = 0.7978845608 + (0.7978845608 * 0.044715) * square
                half = 0.5 + 0.5 * jnp.tanh(p * inner)
                layer_ref[rows, :] = (p * half).astype(BF)
                tail = (2.0 * 0.7978845608) + (6.0 * 0.7978845608 * 0.044715) * square
                slope = half + half * (1.0 - half) * (p * tail)
                grad = (cot_ref[rows, :].astype(F32) * slope).astype(BF)
                pre_ref[rows, :] = grad
                cat_ref[pair & 1, t * NY : (t + 1) * NY, z * BC : (z + 1) * BC] = grad

    def steps(pair, carry):
        step(pair)
        return carry

    step(0, first=True)
    tables[1].wait()
    lax.fori_loop(1, PAIRS - 3, steps, 0, unroll=2)
    step(PAIRS - 3)
    step(PAIRS - 2, final=True)
    step(PAIRS - 1, final=True)
    forward(PAIRS - 1)


def middle(recv, x, cot, inv, fwd, mix, bias):
    cells = (ZL * XL * NY, BC)
    flat = jax.ShapeDtypeStruct(cells, BF)
    return call(
        middle_kernel,
        [jax.ShapeDtypeStruct((MY, PAIRS * ROWS, BC), BF), flat, flat],
        [VMEM] + [REMOTE] * 4 + [VMEM] * 2,
        [VMEM] * 3,
        [
            pltpu.VMEM(cells, BF),
            pltpu.VMEM(cells, BF),
            pltpu.VMEM(inv.shape, BF),
            pltpu.VMEM(fwd.shape, BF),
            pltpu.VMEM((2, PLANE, ZP * BC), BF),
            pltpu.SemaphoreType.DMA((PAIRS,)),
            pltpu.SemaphoreType.DMA((PAIRS,)),
            pltpu.SemaphoreType.DMA((2,)),
        ],
        "middle",
        2 << 29,
        12 << 20,
    )(recv, far(x), far(cot), far(inv), far(fwd), mix, bias)


def last_kernel(recv_ref, pre_ref, inv_ref, mix_ref, out_ref, in_ref, made_ref, wide_ref, in_sem, sem):
    fetches = [
        pltpu.make_async_copy(rows_of(pre_ref, i), in_ref.at[i], in_sem.at[i]) for i in range(STEPS)
    ]
    for copy in fetches[:2]:
        copy.start()
    copies = []
    for i in range(STEPS):
        for j in range(2):
            pair = 2 * i + j
            modes = split_pair(recv_ref[:, pair * ROWS : (pair + 1) * ROWS, :])
            cells = dot(modes, inv_ref[...], ((0,), (0,)))
            if j == 0:
                fetches[i].wait()
                if i + 2 < STEPS:
                    fetches[i + 2].start()
            rows = in_ref[i, j * ZP * PLANE : (j + 1) * ZP * PLANE, :]
            local = dot(mix_ref[...], rows, ((1,), (1,)))
            for z in range(ZP):
                for t in range(XL):
                    at = z * XL + t
                    wide_ref[i % 2, pl.ds(j * CELLS + at, BC, stride=STEP_CELLS), :] = (
                        cells[z * BC : (z + 1) * BC, t * NY : (t + 1) * NY]
                        + local[:, at * NY : (at + 1) * NY]
                    )
        made_ref[i] = wide_ref[i % 2].reshape(BC, STEP_CELLS, NY).astype(BF)
        copies.append(pltpu.make_async_copy(made_ref.at[i], chunk_of(out_ref, i), sem.at[i]))
        copies[i].start()
    for copy in copies:
        copy.wait()


def last(recv, pre, inv, mix):
    return call(
        last_kernel,
        jax.ShapeDtypeStruct((BC, ZL * XL, NY), BF),
        [VMEM, REMOTE, VMEM, VMEM],
        REMOTE,
        [
            pltpu.VMEM((STEPS, STEP_CELLS * NY, BC), BF),
            pltpu.VMEM((STEPS, BC, STEP_CELLS, NY), BF),
            pltpu.VMEM((2, BC * STEP_CELLS, NY), F32),
            pltpu.SemaphoreType.DMA((STEPS,)),
            pltpu.SemaphoreType.DMA((STEPS,)),
        ],
        "last",
        2 << 29,
        8 << 20,
    )(recv, far(pre), inv, mix)


def exchange(x, axis):
    return lax.all_to_all(x, axis, split_axis=0, concat_axis=0, tiled=True)


KX = MX // GZ


def z_forward(recv, table):
    modes = dot(table, recv.reshape(GZ * PAIRS * ROWS, BC))
    return modes.astype(BF).reshape(2, KX, MZ, BATCH, C)


def z_inverse(modes, table):
    return dot(table, modes.reshape(2 * KX * MZ, BC)).astype(BF).reshape(GZ, PAIRS * ROWS, BC)


def body(features, cotangent, spectral, pointwise, channel_bias):
    t = {k: jnp.asarray(v) for k, v in tables().items()}
    x = features.reshape(BC, ZL * XL, NY)
    cot = cotangent.reshape(BC, ZL * XL, NY)
    weights = spectral[0]
    mix = jnp.zeros((BATCH, C, BATCH, C), BF)
    mix = mix.at[0, :, 0, :].set(pointwise).at[1, :, 1, :].set(pointwise).reshape(BC, BC)
    bias = jnp.tile(channel_bias, BATCH)[None, :]

    recv = exchange(y_first(x, t["unit"]), "xy")
    x_lanes = to_lanes(x)
    recv = exchange(x_transform(recv, t["x_fwd"], GZ, FORWARD, "x_forward"), "gz")
    spectra = z_forward(recv, t["z_fwd"])
    products = jnp.einsum("rkmbi,kmio->rkmbo", spectra, weights, preferred_element_type=F32)
    mixed = jnp.stack(
        [
            products[0, ..., :C] - products[1, ..., C:],
            products[0, ..., C:] + products[1, ..., :C],
        ]
    ).astype(BF)
    recv = exchange(z_inverse(mixed, t["z_inv"]), "gz")
    recv = exchange(x_transform(recv, t["x_inv"], XY, INVERSE, "x_inverse"), "xy")
    cot_lanes = to_lanes(cot)
    send, layer, pre = middle(
        recv, x_lanes, cot_lanes, t["doubled_t"], t["doubled"], mix, bias
    )
    recv = exchange(send, "xy")
    layer_out = from_lanes(layer)
    recv = exchange(x_transform(recv, t["x_fwd"], GZ, INVERSE, "x_forward"), "gz")
    mode_grad = z_forward(recv, t["z_fwd"])
    real, imag = mode_grad[0], mode_grad[1]
    paired = jnp.stack(
        [
            jnp.concatenate([real, imag], axis=-1),
            jnp.concatenate([imag, -real], axis=-1),
        ]
    )
    spectra_grad = jnp.einsum(
        "rkmbo,kmio->rkmbi", paired, weights, preferred_element_type=F32
    ).astype(BF)
    recv = exchange(z_inverse(spectra_grad, t["z_inv"]), "gz")
    recv = exchange(x_transform(recv, t["x_inv"], XY, FORWARD, "x_inverse"), "xy")
    spectral_grad = jnp.einsum(
        "rkmbi,rkmbo->kmio", spectra, paired, preferred_element_type=F32
    ).astype(BF)
    input_grad = last(recv, pre, t["unit"], mix)
    return (
        layer_out.reshape(features.shape),
        input_grad.reshape(features.shape),
        spectral_grad[None],
    )


def solution(mesh):
    field = P(None, None, "gz", "xy", None)
    modes = P("xy", "gz", None, None, None)
    return jax.shard_map(
        body,
        mesh=mesh,
        in_specs=(field, field, modes, P(), P()),
        out_specs=(field, field, modes),
        check_vma=False,
    )
```

```python
import functools
import math

import jax
import jax.numpy as jnp
import ml_dtypes
import numpy as np
from jax import lax
from jax.experimental import pallas as pl
from jax.experimental.pallas import tpu as pltpu
from jax.sharding import PartitionSpec as P

C = 64
NX = 128
NY = 128
NZ = 128
MX = 32
MY = 32
MZ = 32
BATCH = 2
GZ = 8
XY = 32
BC = BATCH * C
ZL = NZ // GZ
XL = NX // XY
ZP = 2
PAIRS = ZL // ZP
SUB = 2 * XL
ROWS = ZP * SUB
BF = jnp.bfloat16
F32 = jnp.float32
FORWARD = (NX * NY * NZ) ** (-0.5)
INVERSE = 0.5 * (MX * MY * MZ) ** (-0.5)


def rounded(values):
    return values.astype(np.float32).astype(ml_dtypes.bfloat16).astype(np.float32)


def cos_sin(length, modes, folded):
    freq = np.arange(modes)
    if folded:
        freq = np.where(freq < modes // 2, freq, length - modes + freq)
    phase = (np.arange(length)[:, None] * freq[None, :]) % length
    angle = phase.astype(np.float32) * np.float32(2.0 * math.pi / length)
    return rounded(np.cos(angle)), rounded(np.sin(angle))


@functools.lru_cache(maxsize=None)
def tables():
    cy, sy = cos_sin(NY, MY, False)
    cx, sx = cos_sin(NX, MX, True)
    cz, sz = cos_sin(NZ, MZ, True)
    same = np.eye(XL, dtype=np.float32)
    part = np.stack([cy, -sy])
    unit = np.einsum("ryk,xv->krxvy", part, same).reshape(MY * SUB, XL * NY)
    scale = np.where(np.arange(MY) == 0, 1.0, 2.0).astype(np.float32)
    doubled = unit * np.repeat(scale, SUB)[:, None]
    z2 = np.eye(ZP, dtype=np.float32)
    fx = np.stack([np.stack([cx, sx]), np.stack([-sx, cx])])
    fx = fx.reshape(2, 2, XY, XL, MX)
    x_fwd = np.einsum("sopvk,zw->kszpwov", fx, z2).reshape(MX * 2 * ZP, XY * ROWS)
    gx = np.stack([np.stack([cx, -sx]), np.stack([sx, cx])])
    gx = gx.reshape(2, 2, XY, XL, MX)
    x_inv = np.einsum("sopvk,zw->pzsvkow", gx, z2).reshape(XY * ROWS, MX * 2 * ZP)
    kx = MX // GZ
    kxe = np.eye(kx, dtype=np.float32)
    fz = np.stack([np.stack([cz, sz]), np.stack([-sz, cz])])
    fz = fz.reshape(2, 2, GZ, PAIRS, ZP, MZ)
    z_fwd = np.einsum("sogjzm,kl->skmgjloz", fz, kxe).reshape(2 * kx * MZ, GZ * PAIRS * kx * 2 * ZP)
    gz = np.stack([np.stack([cz, -sz]), np.stack([sz, cz])])
    gz = gz.reshape(2, 2, GZ, PAIRS, ZP, MZ)
    z_inv = np.einsum("sogjzm,kl->gjkszolm", gz, kxe).reshape(GZ * PAIRS * kx * 2 * ZP, 2 * kx * MZ)
    made = dict(
        unit=unit,
        doubled=doubled,
        doubled_t=doubled.T,
        x_fwd=x_fwd,
        x_inv=x_inv,
        z_fwd=z_fwd,
        z_inv=z_inv,
    )
    return {k: np.ascontiguousarray(v).astype(ml_dtypes.bfloat16) for k, v in made.items()}


def dot(a, b, dims=((1,), (0,))):
    return lax.dot_general(a, b, (dims, ((), ())), preferred_element_type=F32)


VM = 24 * 1024 * 1024
STEPS = PAIRS // 2
CELLS = ZP * XL
STEP_CELLS = 2 * CELLS
PLANE = XL * NY
VMEM = pl.BlockSpec(memory_space=pltpu.VMEM)
REMOTE = pl.BlockSpec(memory_space=pltpu.HBM)


def far(x):
    return pltpu.with_memory_space_constraint(x, pltpu.HBM)


def call(kernel, outs, in_specs, out_specs, scratch, name, flops, nbytes):
    return pl.pallas_call(
        kernel,
        out_shape=outs,
        in_specs=in_specs,
        out_specs=out_specs,
        scratch_shapes=scratch,
        name=name,
        compiler_params=pltpu.CompilerParams(vmem_limit_bytes=VM),
        cost_estimate=pl.CostEstimate(flops=flops, bytes_accessed=nbytes, transcendentals=0),
    )


def split_pair(block):
    wide = block.astype(F32)
    n = wide.shape[0]
    halves = [wide[:, z * SUB : (z + 1) * SUB, :].reshape(n * SUB, BC) for z in range(ZP)]
    return jnp.concatenate(halves, axis=1).astype(BF)


def join_pair(wide):
    n = wide.shape[0] // SUB
    halves = [wide[:, z * BC : (z + 1) * BC].reshape(n, SUB, BC) for z in range(ZP)]
    return jnp.concatenate(halves, axis=1).astype(BF)


def chunk_of(ref, step):
    return ref.at[:, step * STEP_CELLS : (step + 1) * STEP_CELLS, :]


def aligned(index, size):
    if isinstance(index, int):
        return index * size
    return pl.multiple_of(index * size, size)


def rows_of(ref, step):
    return ref.at[step * STEP_CELLS * NY : (step + 1) * STEP_CELLS * NY, :]


def first_kernel(x_ref, far_ref, out_ref, in_ref, table_ref, wide_ref, sem):
    cells = [pl.ds(0, STEP_CELLS), pl.ds(STEP_CELLS, ZL * XL - STEP_CELLS)]
    copies = [
        pltpu.make_async_copy(x_ref.at[:, part, :], in_ref.at[:, part, :], sem.at[k])
        for k, part in enumerate(cells)
    ]
    fetch = pltpu.make_async_copy(far_ref, table_ref, sem.at[2])
    copies[0].start()
    fetch.start()
    copies[1].start()
    for i in range(STEPS):
        if i < 2:
            copies[i].wait()
        if i == 0:
            fetch.wait()
        wide_ref[i % 2] = in_ref[:, i * STEP_CELLS : (i + 1) * STEP_CELLS, :].astype(F32).reshape(BC * STEP_CELLS, NY)
        for j in range(2):
            planes = []
            for z in range(ZP):
                cells = [
                    wide_ref[i % 2, pl.ds(j * CELLS + z * XL + t, BC, stride=STEP_CELLS), :].astype(BF)
                    for t in range(XL)
                ]
                planes.append(jnp.concatenate(cells, axis=1))
            both = jnp.concatenate(planes, axis=0)
            modes = dot(table_ref[...], both, ((1,), (1,)))
            at = (2 * i + j) * ROWS
            out_ref[:, at : at + ROWS, :] = join_pair(modes)


def y_first(x, table):
    return call(
        first_kernel,
        jax.ShapeDtypeStruct((MY, PAIRS * ROWS, BC), BF),
        [REMOTE, REMOTE],
        VMEM,
        [
            pltpu.VMEM((BC, ZL * XL, NY), BF),
            pltpu.VMEM(table.shape, BF),
            pltpu.VMEM((2, BC * STEP_CELLS, NY), F32),
            pltpu.SemaphoreType.DMA((3,)),
        ],
        "y_first",
        1 << 29,
        4 << 20,
    )(far(x), far(table))


def to_lanes_kernel(x_ref, out_ref, in_ref, made_ref, wide_ref, sem, out_sem):
    copies = [
        pltpu.make_async_copy(chunk_of(x_ref, i), in_ref.at[i], sem.at[i]) for i in range(STEPS)
    ]
    for copy in copies:
        copy.start()
    outs = []
    for i in range(STEPS):
        copies[i].wait()
        wide_ref[i % 2] = in_ref[i].astype(F32).reshape(BC * STEP_CELLS, NY)
        for t in range(STEP_CELLS):
            cell = wide_ref[i % 2, pl.ds(t, BC, stride=STEP_CELLS), :]
            made_ref[i, t * NY : (t + 1) * NY, :] = cell.T.astype(BF)
        outs.append(pltpu.make_async_copy(made_ref.at[i], rows_of(out_ref, i), out_sem.at[i]))
        outs[i].start()
    for copy in outs:
        copy.wait()


def to_lanes(x):
    return call(
        to_lanes_kernel,
        jax.ShapeDtypeStruct((ZL * XL * NY, BC), BF),
        [REMOTE],
        REMOTE,
        [
            pltpu.VMEM((STEPS, BC, STEP_CELLS, NY), BF),
            pltpu.VMEM((STEPS, STEP_CELLS * NY, BC), BF),
            pltpu.VMEM((2, BC * STEP_CELLS, NY), F32),
            pltpu.SemaphoreType.DMA((STEPS,)),
            pltpu.SemaphoreType.DMA((STEPS,)),
        ],
        "to_lanes",
        0,
        12 << 20,
    )(far(x))


def from_lanes_kernel(x_ref, out_ref, in_ref, made_ref, wide_ref, in_sem, sem):
    fetches = [
        pltpu.make_async_copy(rows_of(x_ref, i), in_ref.at[i], in_sem.at[i]) for i in range(STEPS)
    ]
    for copy in fetches:
        copy.start()
    copies = []
    for i in range(STEPS):
        fetches[i].wait()
        for t in range(STEP_CELLS):
            cell = in_ref[i, t * NY : (t + 1) * NY, :].astype(F32)
            wide_ref[i % 2, pl.ds(t, BC, stride=STEP_CELLS), :] = cell.T
        made_ref[i] = wide_ref[i % 2].reshape(BC, STEP_CELLS, NY).astype(BF)
        copies.append(pltpu.make_async_copy(made_ref.at[i], chunk_of(out_ref, i), sem.at[i]))
        copies[i].start()
    for copy in copies:
        copy.wait()


def from_lanes(x):
    return call(
        from_lanes_kernel,
        jax.ShapeDtypeStruct((BC, ZL * XL, NY), BF),
        [REMOTE],
        REMOTE,
        [
            pltpu.VMEM((STEPS, STEP_CELLS * NY, BC), BF),
            pltpu.VMEM((STEPS, BC, STEP_CELLS, NY), BF),
            pltpu.VMEM((2, BC * STEP_CELLS, NY), F32),
            pltpu.SemaphoreType.DMA((STEPS,)),
            pltpu.SemaphoreType.DMA((STEPS,)),
        ],
        "from_lanes",
        0,
        12 << 20,
    )(far(x))


def x_kernel(groups_in, groups_out, scale, recv_ref, table_ref, out_ref, made_ref=None, sem=None):
    target = out_ref if made_ref is None else made_ref
    copies = []
    for i in range(STEPS):
        wide = jnp.concatenate(
            [
                recv_ref[:, (2 * i + j) * ROWS : (2 * i + j + 1) * ROWS, :].reshape(
                    groups_in * ROWS, BC
                )
                for j in range(2)
            ],
            axis=1,
        )
        done = (dot(table_ref[...], wide) * scale).astype(BF)
        for j in range(2):
            at = (2 * i + j) * ROWS
            target[:, at : at + ROWS, :] = done[:, j * BC : (j + 1) * BC].reshape(
                groups_out, ROWS, BC
            )
        if made_ref is not None and i % 2 == 1:
            rows = pl.ds((i - 1) * 2 * ROWS, 4 * ROWS)
            copies.append(
                pltpu.make_async_copy(made_ref.at[:, rows, :], out_ref.at[:, rows, :], sem.at[i // 2])
            )
            copies[-1].start()
    for copy in copies:
        copy.wait()


def x_transform(recv, table, groups_out, scale, name, away=False):
    shape = (groups_out, PAIRS * ROWS, BC)
    return call(
        functools.partial(x_kernel, recv.shape[0], groups_out, scale),
        jax.ShapeDtypeStruct(shape, BF),
        [VMEM, VMEM],
        REMOTE if away else VMEM,
        [pltpu.VMEM(shape, BF), pltpu.SemaphoreType.DMA((STEPS // 2,))] if away else [],
        name,
        1 << 27,
        2 << 20,
    )(recv, table)


GROUPS = ((0, 1), (1, 3), (3, PAIRS))


def middle_kernel(
    recv_ref,
    x_far,
    cot_far,
    inv_far,
    fwd_far,
    mix_ref,
    bias_ref,
    send_ref,
    layer_ref,
    pre_ref,
    x_ref,
    cot_ref,
    inv_ref,
    fwd_ref,
    cat_ref,
    x_sem,
    cot_sem,
    table_sem,
):
    depth = ZP * PLANE

    def moves(group):
        low, high = GROUPS[group]
        rows = pl.ds(low * depth, (high - low) * depth)
        return [
            pltpu.make_async_copy(source.at[rows, :], target.at[rows, :], sem.at[group])
            for source, target, sem in ((x_far, x_ref, x_sem), (cot_far, cot_ref, cot_sem))
        ]

    tables = [
        pltpu.make_async_copy(inv_far, inv_ref, table_sem.at[0]),
        pltpu.make_async_copy(fwd_far, fwd_ref, table_sem.at[1]),
    ]

    tables[0].start()
    for group in range(len(GROUPS)):
        for move in moves(group):
            move.start()
        if group == 0:
            tables[1].start()

    def forward(pair):
        modes = dot(fwd_ref[...], cat_ref[pair & 1])
        send_ref[:, pl.ds(aligned(pair, ROWS), ROWS), :] = join_pair(modes)

    mix = mix_ref[...]
    none = jnp.zeros_like(mix)
    lower = jnp.concatenate(
        [jnp.concatenate([mix, none], axis=1), jnp.concatenate([none, mix], axis=1)], axis=0
    )
    bias = bias_ref[...]

    tables[0].wait()

    def step(pair, first=False):
        if not first:
            forward(pair - 1)
        block = recv_ref[:, pl.ds(aligned(pair, ROWS), ROWS), :]
        right = jnp.concatenate([split_pair(block), lower], axis=0)
        base = aligned(pair, depth)
        for t in range(XL):
            cells = [pl.ds(base + z * PLANE + t * NY, NY) for z in range(ZP)]
            left = jnp.concatenate(
                [inv_ref[t * NY : (t + 1) * NY, :]] + [x_ref[rows, :] for rows in cells], axis=1
            )
            total = dot(left, right)
            for z, rows in enumerate(cells):
                p = total[:, z * BC : (z + 1) * BC] + bias
                square = p * p
                inner = 0.7978845608 + (0.7978845608 * 0.044715) * square
                half = 0.5 + 0.5 * jnp.tanh(p * inner)
                layer_ref[rows, :] = (p * half).astype(BF)
                tail = (2.0 * 0.7978845608) + (6.0 * 0.7978845608 * 0.044715) * square
                slope = half + half * (1.0 - half) * (p * tail)
                grad = (cot_ref[rows, :].astype(F32) * slope).astype(BF)
                pre_ref[rows, :] = grad
                cat_ref[pair & 1, t * NY : (t + 1) * NY, z * BC : (z + 1) * BC] = grad

    def steps(pair, carry):
        step(pair)
        return carry

    for group, (low, high) in enumerate(GROUPS):
        for move in moves(group):
            move.wait()
        if low == 0:
            step(0, first=True)
            tables[1].wait()
            low = 1
        if high - low > 1:
            lax.fori_loop(low, high - (high - low) % 2, steps, 0, unroll=2)
        if (high - low) % 2:
            step(high - 1)
    forward(PAIRS - 1)


def middle(recv, x, cot, inv, fwd, mix, bias):
    cells = (ZL * XL * NY, BC)
    flat = jax.ShapeDtypeStruct(cells, BF)
    return call(
        middle_kernel,
        [jax.ShapeDtypeStruct((MY, PAIRS * ROWS, BC), BF), flat, flat],
        [VMEM] + [REMOTE] * 4 + [VMEM] * 2,
        [VMEM] * 3,
        [
            pltpu.VMEM(cells, BF),
            pltpu.VMEM(cells, BF),
            pltpu.VMEM(inv.shape, BF),
            pltpu.VMEM(fwd.shape, BF),
            pltpu.VMEM((2, PLANE, ZP * BC), BF),
            pltpu.SemaphoreType.DMA((len(GROUPS),)),
            pltpu.SemaphoreType.DMA((len(GROUPS),)),
            pltpu.SemaphoreType.DMA((2,)),
        ],
        "middle",
        2 << 29,
        12 << 20,
    )(recv, far(x), far(cot), far(inv), far(fwd), mix, bias)


def halves(source, target, sem):
    cut = STEP_CELLS * NY
    parts = [pl.ds(0, cut), pl.ds(cut, ZL * XL * NY - cut)]
    return [
        pltpu.make_async_copy(source.at[rows, :], target.at[rows, :], sem.at[k])
        for k, rows in enumerate(parts)
    ]


def last_kernel(recv_ref, pre_ref, inv_ref, mix_ref, out_ref, in_ref, made_ref, wide_ref, in_sem, sem):
    fetches = halves(pre_ref, in_ref, in_sem)
    for copy in fetches:
        copy.start()
    copies = []
    for i in range(STEPS):
        for j in range(2):
            pair = 2 * i + j
            modes = split_pair(recv_ref[:, pair * ROWS : (pair + 1) * ROWS, :])
            cells = dot(modes, inv_ref[...], ((0,), (0,)))
            if j == 0 and i < len(fetches):
                fetches[i].wait()
            at = pair * ZP * PLANE
            rows = in_ref[at : at + ZP * PLANE, :]
            local = dot(mix_ref[...], rows, ((1,), (1,)))
            for z in range(ZP):
                for t in range(XL):
                    at = z * XL + t
                    wide_ref[i % 2, pl.ds(j * CELLS + at, BC, stride=STEP_CELLS), :] = (
                        cells[z * BC : (z + 1) * BC, t * NY : (t + 1) * NY]
                        + local[:, at * NY : (at + 1) * NY]
                    )
        made_ref[i] = wide_ref[i % 2].reshape(BC, STEP_CELLS, NY).astype(BF)
        copies.append(pltpu.make_async_copy(made_ref.at[i], chunk_of(out_ref, i), sem.at[i]))
        copies[i].start()
    for copy in copies:
        copy.wait()


def last(recv, pre, inv, mix):
    return call(
        last_kernel,
        jax.ShapeDtypeStruct((BC, ZL * XL, NY), BF),
        [VMEM, REMOTE, VMEM, VMEM],
        REMOTE,
        [
            pltpu.VMEM((ZL * XL * NY, BC), BF),
            pltpu.VMEM((STEPS, BC, STEP_CELLS, NY), BF),
            pltpu.VMEM((2, BC * STEP_CELLS, NY), F32),
            pltpu.SemaphoreType.DMA((2,)),
            pltpu.SemaphoreType.DMA((STEPS,)),
        ],
        "last",
        2 << 29,
        8 << 20,
    )(recv, far(pre), inv, mix)


def exchange(x, axis):
    return lax.all_to_all(x, axis, split_axis=0, concat_axis=0, tiled=True)


KX = MX // GZ


def z_forward(recv, table):
    modes = dot(table, recv.reshape(GZ * PAIRS * ROWS, BC))
    return modes.astype(BF).reshape(2, KX, MZ, BATCH, C)


def z_inverse(modes, table):
    return dot(table, modes.reshape(2 * KX * MZ, BC)).astype(BF).reshape(GZ, PAIRS * ROWS, BC)


def body(features, cotangent, spectral, pointwise, channel_bias):
    t = {k: jnp.asarray(v) for k, v in tables().items()}
    x = features.reshape(BC, ZL * XL, NY)
    cot = cotangent.reshape(BC, ZL * XL, NY)
    weights = spectral[0]
    mix = jnp.zeros((BATCH, C, BATCH, C), BF)
    mix = mix.at[0, :, 0, :].set(pointwise).at[1, :, 1, :].set(pointwise).reshape(BC, BC)
    bias = jnp.tile(channel_bias, BATCH)[None, :]

    recv = exchange(y_first(x, t["unit"]), "xy")
    x_lanes = to_lanes(x)
    recv = exchange(x_transform(recv, t["x_fwd"], GZ, FORWARD, "x_forward"), "gz")
    spectra = z_forward(recv, t["z_fwd"])
    products = jnp.einsum("rkmbi,kmio->rkmbo", spectra, weights, preferred_element_type=F32)
    mixed = jnp.stack(
        [
            products[0, ..., :C] - products[1, ..., C:],
            products[0, ..., C:] + products[1, ..., :C],
        ]
    ).astype(BF)
    recv = exchange(z_inverse(mixed, t["z_inv"]), "gz")
    recv = exchange(x_transform(recv, t["x_inv"], XY, INVERSE, "x_inverse", True), "xy")
    cot_lanes = to_lanes(cot)
    send, layer, pre = middle(
        recv, x_lanes, cot_lanes, t["doubled_t"], t["doubled"], mix, bias
    )
    recv = exchange(send, "xy")
    layer_out = from_lanes(layer)
    recv = exchange(x_transform(recv, t["x_fwd"], GZ, INVERSE, "x_forward"), "gz")
    mode_grad = z_forward(recv, t["z_fwd"])
    real, imag = mode_grad[0], mode_grad[1]
    paired = jnp.stack(
        [
            jnp.concatenate([real, imag], axis=-1),
            jnp.concatenate([imag, -real], axis=-1),
        ]
    )
    spectra_grad = jnp.einsum(
        "rkmbo,kmio->rkmbi", paired, weights, preferred_element_type=F32
    ).astype(BF)
    recv = exchange(z_inverse(spectra_grad, t["z_inv"]), "gz")
    recv = exchange(x_transform(recv, t["x_inv"], XY, FORWARD, "x_inverse", True), "xy")
    spectral_grad = jnp.einsum(
        "rkmbi,rkmbo->kmio", spectra, paired, preferred_element_type=F32
    ).astype(BF)
    input_grad = last(recv, pre, t["unit"], mix)
    return (
        layer_out.reshape(features.shape),
        input_grad.reshape(features.shape),
        spectral_grad[None],
    )


def solution(mesh):
    field = P(None, None, "gz", "xy", None)
    modes = P("xy", "gz", None, None, None)
    return jax.shard_map(
        body,
        mesh=mesh,
        in_specs=(field, field, modes, P(), P()),
        out_specs=(field, field, modes),
        check_vma=False,
    )
```

```python
import functools
import math

import jax
import jax.numpy as jnp
import ml_dtypes
import numpy as np
from jax import lax
from jax.experimental import pallas as pl
from jax.experimental.pallas import tpu as pltpu
from jax.sharding import PartitionSpec as P

C = 64
NX = 128
NY = 128
NZ = 128
MX = 32
MY = 32
MZ = 32
BATCH = 2
GZ = 8
XY = 32
BC = BATCH * C
ZL = NZ // GZ
XL = NX // XY
ZP = 2
PAIRS = ZL // ZP
SUB = 2 * XL
ROWS = ZP * SUB
BF = jnp.bfloat16
F32 = jnp.float32
FORWARD = (NX * NY * NZ) ** (-0.5)
INVERSE = 0.5 * (MX * MY * MZ) ** (-0.5)


def rounded(values):
    return values.astype(np.float32).astype(ml_dtypes.bfloat16).astype(np.float32)


def cos_sin(length, modes, folded):
    freq = np.arange(modes)
    if folded:
        freq = np.where(freq < modes // 2, freq, length - modes + freq)
    phase = (np.arange(length)[:, None] * freq[None, :]) % length
    angle = phase.astype(np.float32) * np.float32(2.0 * math.pi / length)
    return rounded(np.cos(angle)), rounded(np.sin(angle))


@functools.lru_cache(maxsize=None)
def tables():
    cy, sy = cos_sin(NY, MY, False)
    cx, sx = cos_sin(NX, MX, True)
    cz, sz = cos_sin(NZ, MZ, True)
    same = np.eye(XL, dtype=np.float32)
    part = np.stack([cy, -sy])
    unit = np.einsum("ryk,xv->krxvy", part, same).reshape(MY * SUB, XL * NY)
    scale = np.where(np.arange(MY) == 0, 1.0, 2.0).astype(np.float32)
    doubled = unit * np.repeat(scale, SUB)[:, None]
    z2 = np.eye(ZP, dtype=np.float32)
    fx = np.stack([np.stack([cx, sx]), np.stack([-sx, cx])])
    fx = fx.reshape(2, 2, XY, XL, MX)
    x_fwd = np.einsum("sopvk,zw->kszpwov", fx, z2).reshape(MX * 2 * ZP, XY * ROWS)
    gx = np.stack([np.stack([cx, -sx]), np.stack([sx, cx])])
    gx = gx.reshape(2, 2, XY, XL, MX)
    x_inv = np.einsum("sopvk,zw->pzsvkow", gx, z2).reshape(XY * ROWS, MX * 2 * ZP)
    kx = MX // GZ
    kxe = np.eye(kx, dtype=np.float32)
    fz = np.stack([np.stack([cz, sz]), np.stack([-sz, cz])])
    fz = fz.reshape(2, 2, GZ, PAIRS, ZP, MZ)
    z_fwd = np.einsum("sogjzm,kl->skmgjloz", fz, kxe).reshape(2 * kx * MZ, GZ * PAIRS * kx * 2 * ZP)
    gz = np.stack([np.stack([cz, -sz]), np.stack([sz, cz])])
    gz = gz.reshape(2, 2, GZ, PAIRS, ZP, MZ)
    z_inv = np.einsum("sogjzm,kl->gjkszolm", gz, kxe).reshape(GZ * PAIRS * kx * 2 * ZP, 2 * kx * MZ)
    made = dict(
        unit=unit,
        doubled=doubled,
        doubled_t=doubled.T,
        x_fwd=x_fwd,
        x_inv=x_inv,
        z_fwd=z_fwd,
        z_inv=z_inv,
    )
    return {k: np.ascontiguousarray(v).astype(ml_dtypes.bfloat16) for k, v in made.items()}


def dot(a, b, dims=((1,), (0,))):
    return lax.dot_general(a, b, (dims, ((), ())), preferred_element_type=F32)


VM = 24 * 1024 * 1024
STEPS = PAIRS // 2
CELLS = ZP * XL
STEP_CELLS = 2 * CELLS
PLANE = XL * NY
VMEM = pl.BlockSpec(memory_space=pltpu.VMEM)
REMOTE = pl.BlockSpec(memory_space=pltpu.HBM)


def far(x):
    return pltpu.with_memory_space_constraint(x, pltpu.HBM)


def call(kernel, outs, in_specs, out_specs, scratch, name, flops, nbytes):
    return pl.pallas_call(
        kernel,
        out_shape=outs,
        in_specs=in_specs,
        out_specs=out_specs,
        scratch_shapes=scratch,
        name=name,
        compiler_params=pltpu.CompilerParams(vmem_limit_bytes=VM),
        cost_estimate=pl.CostEstimate(flops=flops, bytes_accessed=nbytes, transcendentals=0),
    )


def split_pair(block):
    wide = block.astype(F32)
    n = wide.shape[0]
    halves = [wide[:, z * SUB : (z + 1) * SUB, :].reshape(n * SUB, BC) for z in range(ZP)]
    return jnp.concatenate(halves, axis=1).astype(BF)


def join_pair(wide):
    n = wide.shape[0] // SUB
    halves = [wide[:, z * BC : (z + 1) * BC].reshape(n, SUB, BC) for z in range(ZP)]
    return jnp.concatenate(halves, axis=1).astype(BF)


def chunk_of(ref, step):
    return ref.at[:, step * STEP_CELLS : (step + 1) * STEP_CELLS, :]


def aligned(index, size):
    if isinstance(index, int):
        return index * size
    return pl.multiple_of(index * size, size)


def rows_of(ref, step):
    return ref.at[step * STEP_CELLS * NY : (step + 1) * STEP_CELLS * NY, :]


def first_kernel(x_ref, far_ref, out_ref, in_ref, table_ref, wide_ref, sem):
    cells = [pl.ds(0, STEP_CELLS), pl.ds(STEP_CELLS, ZL * XL - STEP_CELLS)]
    copies = [
        pltpu.make_async_copy(x_ref.at[:, part, :], in_ref.at[:, part, :], sem.at[k])
        for k, part in enumerate(cells)
    ]
    fetch = pltpu.make_async_copy(far_ref, table_ref, sem.at[2])
    copies[0].start()
    fetch.start()
    copies[1].start()
    for i in range(STEPS):
        if i < 2:
            copies[i].wait()
        if i == 0:
            fetch.wait()
        wide_ref[i % 2] = in_ref[:, i * STEP_CELLS : (i + 1) * STEP_CELLS, :].astype(F32).reshape(BC * STEP_CELLS, NY)
        for j in range(2):
            planes = []
            for z in range(ZP):
                cells = [
                    wide_ref[i % 2, pl.ds(j * CELLS + z * XL + t, BC, stride=STEP_CELLS), :].astype(BF)
                    for t in range(XL)
                ]
                planes.append(jnp.concatenate(cells, axis=1))
            both = jnp.concatenate(planes, axis=0)
            modes = dot(table_ref[...], both, ((1,), (1,)))
            at = (2 * i + j) * ROWS
            out_ref[:, at : at + ROWS, :] = join_pair(modes)


def y_first(x, table):
    return call(
        first_kernel,
        jax.ShapeDtypeStruct((MY, PAIRS * ROWS, BC), BF),
        [REMOTE, REMOTE],
        VMEM,
        [
            pltpu.VMEM((BC, ZL * XL, NY), BF),
            pltpu.VMEM(table.shape, BF),
            pltpu.VMEM((2, BC * STEP_CELLS, NY), F32),
            pltpu.SemaphoreType.DMA((3,)),
        ],
        "y_first",
        1 << 29,
        4 << 20,
    )(far(x), far(table))


def to_lanes_kernel(x_ref, out_ref, in_ref, made_ref, wide_ref, sem, out_sem):
    copies = [
        pltpu.make_async_copy(chunk_of(x_ref, i), in_ref.at[i], sem.at[i]) for i in range(STEPS)
    ]
    for copy in copies:
        copy.start()
    outs = []
    for i in range(STEPS):
        copies[i].wait()
        wide_ref[i % 2] = in_ref[i].astype(F32).reshape(BC * STEP_CELLS, NY)
        for t in range(STEP_CELLS):
            cell = wide_ref[i % 2, pl.ds(t, BC, stride=STEP_CELLS), :]
            made_ref[i, t * NY : (t + 1) * NY, :] = cell.T.astype(BF)
        outs.append(pltpu.make_async_copy(made_ref.at[i], rows_of(out_ref, i), out_sem.at[i]))
        outs[i].start()
    for copy in outs:
        copy.wait()


def to_lanes(x):
    return call(
        to_lanes_kernel,
        jax.ShapeDtypeStruct((ZL * XL * NY, BC), BF),
        [REMOTE],
        REMOTE,
        [
            pltpu.VMEM((STEPS, BC, STEP_CELLS, NY), BF),
            pltpu.VMEM((STEPS, STEP_CELLS * NY, BC), BF),
            pltpu.VMEM((2, BC * STEP_CELLS, NY), F32),
            pltpu.SemaphoreType.DMA((STEPS,)),
            pltpu.SemaphoreType.DMA((STEPS,)),
        ],
        "to_lanes",
        0,
        12 << 20,
    )(far(x))


def from_lanes_kernel(x_ref, out_ref, in_ref, made_ref, wide_ref, in_sem, sem):
    fetches = [
        pltpu.make_async_copy(rows_of(x_ref, i), in_ref.at[i], in_sem.at[i]) for i in range(STEPS)
    ]
    for copy in fetches:
        copy.start()
    copies = []
    for i in range(STEPS):
        fetches[i].wait()
        for t in range(STEP_CELLS):
            cell = in_ref[i, t * NY : (t + 1) * NY, :].astype(F32)
            wide_ref[i % 2, pl.ds(t, BC, stride=STEP_CELLS), :] = cell.T
        made_ref[i] = wide_ref[i % 2].reshape(BC, STEP_CELLS, NY).astype(BF)
        copies.append(pltpu.make_async_copy(made_ref.at[i], chunk_of(out_ref, i), sem.at[i]))
        copies[i].start()
    for copy in copies:
        copy.wait()


def from_lanes(x):
    return call(
        from_lanes_kernel,
        jax.ShapeDtypeStruct((BC, ZL * XL, NY), BF),
        [REMOTE],
        REMOTE,
        [
            pltpu.VMEM((STEPS, STEP_CELLS * NY, BC), BF),
            pltpu.VMEM((STEPS, BC, STEP_CELLS, NY), BF),
            pltpu.VMEM((2, BC * STEP_CELLS, NY), F32),
            pltpu.SemaphoreType.DMA((STEPS,)),
            pltpu.SemaphoreType.DMA((STEPS,)),
        ],
        "from_lanes",
        0,
        12 << 20,
    )(far(x))


def x_kernel(groups_in, groups_out, scale, recv_ref, table_ref, out_ref, made_ref=None, sem=None):
    target = out_ref if made_ref is None else made_ref
    copies = []
    for i in range(STEPS):
        wide = jnp.concatenate(
            [
                recv_ref[:, (2 * i + j) * ROWS : (2 * i + j + 1) * ROWS, :].reshape(
                    groups_in * ROWS, BC
                )
                for j in range(2)
            ],
            axis=1,
        )
        done = (dot(table_ref[...], wide) * scale).astype(BF)
        for j in range(2):
            at = (2 * i + j) * ROWS
            target[:, at : at + ROWS, :] = done[:, j * BC : (j + 1) * BC].reshape(
                groups_out, ROWS, BC
            )
        if made_ref is not None and i % 2 == 1:
            rows = pl.ds((i - 1) * 2 * ROWS, 4 * ROWS)
            copies.append(
                pltpu.make_async_copy(made_ref.at[:, rows, :], out_ref.at[:, rows, :], sem.at[i // 2])
            )
            copies[-1].start()
    for copy in copies:
        copy.wait()


def x_transform(recv, table, groups_out, scale, name, away=False):
    shape = (groups_out, PAIRS * ROWS, BC)
    return call(
        functools.partial(x_kernel, recv.shape[0], groups_out, scale),
        jax.ShapeDtypeStruct(shape, BF),
        [VMEM, VMEM],
        REMOTE if away else VMEM,
        [pltpu.VMEM(shape, BF), pltpu.SemaphoreType.DMA((STEPS // 2,))] if away else [],
        name,
        1 << 27,
        2 << 20,
    )(recv, table)


GROUPS = ((0, 1), (1, 3), (3, PAIRS))


def middle_kernel(
    recv_ref,
    x_far,
    cot_far,
    inv_far,
    fwd_far,
    mix_ref,
    bias_ref,
    send_ref,
    layer_ref,
    pre_ref,
    x_ref,
    cot_ref,
    inv_ref,
    fwd_ref,
    cat_ref,
    x_sem,
    cot_sem,
    table_sem,
):
    depth = ZP * PLANE

    def moves(group):
        low, high = GROUPS[group]
        rows = pl.ds(low * depth, (high - low) * depth)
        return [
            pltpu.make_async_copy(source.at[rows, :], target.at[rows, :], sem.at[group])
            for source, target, sem in ((x_far, x_ref, x_sem), (cot_far, cot_ref, cot_sem))
        ]

    tables = [
        pltpu.make_async_copy(inv_far, inv_ref, table_sem.at[0]),
        pltpu.make_async_copy(fwd_far, fwd_ref, table_sem.at[1]),
    ]

    tables[0].start()
    for group in range(len(GROUPS)):
        for move in moves(group):
            move.start()
        if group == 0:
            tables[1].start()

    def forward(pair):
        modes = dot(fwd_ref[...], cat_ref[pair & 1])
        send_ref[:, pl.ds(aligned(pair, ROWS), ROWS), :] = join_pair(modes)

    mix = mix_ref[...]
    none = jnp.zeros_like(mix)
    lower = jnp.concatenate(
        [jnp.concatenate([mix, none], axis=1), jnp.concatenate([none, mix], axis=1)], axis=0
    )
    bias = bias_ref[...]

    tables[0].wait()

    def step(pair, first=False):
        if not first:
            forward(pair - 1)
        block = recv_ref[:, pl.ds(aligned(pair, ROWS), ROWS), :]
        right = jnp.concatenate([split_pair(block), lower], axis=0)
        base = aligned(pair, depth)
        for t in range(XL):
            cells = [pl.ds(base + z * PLANE + t * NY, NY) for z in range(ZP)]
            left = jnp.concatenate(
                [inv_ref[t * NY : (t + 1) * NY, :]] + [x_ref[rows, :] for rows in cells], axis=1
            )
            total = dot(left, right)
            for z, rows in enumerate(cells):
                p = total[:, z * BC : (z + 1) * BC] + bias
                square = p * p
                inner = 0.7978845608 + (0.7978845608 * 0.044715) * square
                half = 0.5 + 0.5 * jnp.tanh(p * inner)
                layer_ref[rows, :] = (p * half).astype(BF)
                tail = (2.0 * 0.7978845608) + (6.0 * 0.7978845608 * 0.044715) * square
                slope = half + half * (1.0 - half) * (p * tail)
                grad = (cot_ref[rows, :].astype(F32) * slope).astype(BF)
                pre_ref[rows, :] = grad
                cat_ref[pair & 1, t * NY : (t + 1) * NY, z * BC : (z + 1) * BC] = grad

    def steps(pair, carry):
        step(pair)
        return carry

    for group, (low, high) in enumerate(GROUPS):
        for move in moves(group):
            move.wait()
        if low == 0:
            step(0, first=True)
            tables[1].wait()
            low = 1
        if high - low > 1:
            lax.fori_loop(low, high - (high - low) % 2, steps, 0, unroll=2)
        if (high - low) % 2:
            step(high - 1)
    forward(PAIRS - 1)


def middle(recv, x, cot, inv, fwd, mix, bias):
    cells = (ZL * XL * NY, BC)
    flat = jax.ShapeDtypeStruct(cells, BF)
    return call(
        middle_kernel,
        [jax.ShapeDtypeStruct((MY, PAIRS * ROWS, BC), BF), flat, flat],
        [VMEM] + [REMOTE] * 4 + [VMEM] * 2,
        [VMEM] * 3,
        [
            pltpu.VMEM(cells, BF),
            pltpu.VMEM(cells, BF),
            pltpu.VMEM(inv.shape, BF),
            pltpu.VMEM(fwd.shape, BF),
            pltpu.VMEM((2, PLANE, ZP * BC), BF),
            pltpu.SemaphoreType.DMA((len(GROUPS),)),
            pltpu.SemaphoreType.DMA((len(GROUPS),)),
            pltpu.SemaphoreType.DMA((2,)),
        ],
        "middle",
        2 << 29,
        12 << 20,
    )(recv, far(x), far(cot), far(inv), far(fwd), mix, bias)


def halves(source, target, sem):
    cut = STEP_CELLS * NY
    parts = [pl.ds(0, cut), pl.ds(cut, ZL * XL * NY - cut)]
    return [
        pltpu.make_async_copy(source.at[rows, :], target.at[rows, :], sem.at[k])
        for k, rows in enumerate(parts)
    ]


def last_kernel(recv_ref, pre_ref, inv_ref, mix_ref, out_ref, in_ref, made_ref, wide_ref, in_sem, sem):
    fetches = halves(pre_ref, in_ref, in_sem)
    for copy in fetches:
        copy.start()
    copies = []
    for i in range(STEPS):
        for j in range(2):
            pair = 2 * i + j
            modes = split_pair(recv_ref[:, pair * ROWS : (pair + 1) * ROWS, :])
            cells = dot(modes, inv_ref[...], ((0,), (0,)))
            if j == 0 and i < len(fetches):
                fetches[i].wait()
            at = pair * ZP * PLANE
            rows = in_ref[at : at + ZP * PLANE, :]
            local = dot(mix_ref[...], rows, ((1,), (1,)))
            for z in range(ZP):
                for t in range(XL):
                    at = z * XL + t
                    wide_ref[i % 2, pl.ds(j * CELLS + at, BC, stride=STEP_CELLS), :] = (
                        cells[z * BC : (z + 1) * BC, t * NY : (t + 1) * NY]
                        + local[:, at * NY : (at + 1) * NY]
                    )
        made_ref[i] = wide_ref[i % 2].reshape(BC, STEP_CELLS, NY).astype(BF)
        copies.append(pltpu.make_async_copy(made_ref.at[i], chunk_of(out_ref, i), sem.at[i]))
        copies[i].start()
    for copy in copies:
        copy.wait()


def last(recv, pre, inv, mix):
    return call(
        last_kernel,
        jax.ShapeDtypeStruct((BC, ZL * XL, NY), BF),
        [VMEM, REMOTE, VMEM, VMEM],
        REMOTE,
        [
            pltpu.VMEM((ZL * XL * NY, BC), BF),
            pltpu.VMEM((STEPS, BC, STEP_CELLS, NY), BF),
            pltpu.VMEM((2, BC * STEP_CELLS, NY), F32),
            pltpu.SemaphoreType.DMA((2,)),
            pltpu.SemaphoreType.DMA((STEPS,)),
        ],
        "last",
        2 << 29,
        8 << 20,
    )(recv, far(pre), inv, mix)


def exchange(x, axis):
    return lax.all_to_all(x, axis, split_axis=0, concat_axis=0, tiled=True)


KX = MX // GZ


def z_forward_kernel(recv_ref, table_ref, real_ref, imag_ref):
    half = KX * MZ
    rows = recv_ref[...].reshape(GZ * PAIRS * ROWS, BC)
    real_ref[...] = dot(table_ref[:half, :], rows).astype(BF)
    imag_ref[...] = dot(table_ref[half:, :], rows).astype(BF)


def z_forward(recv, table):
    part = jax.ShapeDtypeStruct((KX * MZ, BC), BF)
    parts = call(
        z_forward_kernel,
        [part, part],
        [VMEM] * 2,
        [VMEM] * 2,
        [],
        "z_forward",
        1 << 26,
        1 << 20,
    )(recv, table)
    return [x.reshape(KX, MZ, BATCH, C) for x in parts]


def z_inverse_kernel(real_ref, imag_ref, table_ref, out_ref):
    half = KX * MZ
    total = dot(table_ref[:, :half], real_ref[...]) + dot(table_ref[:, half:], imag_ref[...])
    out_ref[...] = total.astype(BF).reshape(GZ, PAIRS * ROWS, BC)


def z_inverse(real, imag, table):
    return call(
        z_inverse_kernel,
        jax.ShapeDtypeStruct((GZ, PAIRS * ROWS, BC), BF),
        [VMEM] * 3,
        VMEM,
        [],
        "z_inverse",
        1 << 26,
        1 << 20,
    )(real.reshape(KX * MZ, BC), imag.reshape(KX * MZ, BC), table)


def body(features, cotangent, spectral, pointwise, channel_bias):
    t = {k: jnp.asarray(v) for k, v in tables().items()}
    x = features.reshape(BC, ZL * XL, NY)
    cot = cotangent.reshape(BC, ZL * XL, NY)
    weights = spectral[0]
    mix = jnp.zeros((BATCH, C, BATCH, C), BF)
    mix = mix.at[0, :, 0, :].set(pointwise).at[1, :, 1, :].set(pointwise).reshape(BC, BC)
    bias = jnp.tile(channel_bias, BATCH)[None, :]

    recv = exchange(y_first(x, t["unit"]), "xy")
    x_lanes = to_lanes(x)
    recv = exchange(x_transform(recv, t["x_fwd"], GZ, FORWARD, "x_forward"), "gz")
    spectra = jnp.stack(z_forward(recv, t["z_fwd"]))
    products = jnp.einsum("rkmbi,kmio->rkmbo", spectra, weights, preferred_element_type=F32)
    real = (products[0, ..., :C] - products[1, ..., C:]).astype(BF)
    imag = (products[0, ..., C:] + products[1, ..., :C]).astype(BF)
    recv = exchange(z_inverse(real, imag, t["z_inv"]), "gz")
    recv = exchange(x_transform(recv, t["x_inv"], XY, INVERSE, "x_inverse", True), "xy")
    cot_lanes = to_lanes(cot)
    send, layer, pre = middle(
        recv, x_lanes, cot_lanes, t["doubled_t"], t["doubled"], mix, bias
    )
    recv = exchange(send, "xy")
    layer_out = from_lanes(layer)
    recv = exchange(x_transform(recv, t["x_fwd"], GZ, INVERSE, "x_forward"), "gz")
    real, imag = z_forward(recv, t["z_fwd"])
    paired = jnp.stack(
        [
            jnp.concatenate([real, imag], axis=-1),
            jnp.concatenate([imag, -real], axis=-1),
        ]
    )
    spectra_grad = jnp.einsum(
        "rkmbo,kmio->rkmbi", paired, weights, preferred_element_type=F32
    ).astype(BF)
    recv = exchange(z_inverse(spectra_grad[0], spectra_grad[1], t["z_inv"]), "gz")
    recv = exchange(x_transform(recv, t["x_inv"], XY, FORWARD, "x_inverse", True), "xy")
    spectral_grad = jnp.einsum(
        "rkmbi,rkmbo->kmio", spectra, paired, preferred_element_type=F32
    ).astype(BF)
    input_grad = last(recv, pre, t["unit"], mix)
    return (
        layer_out.reshape(features.shape),
        input_grad.reshape(features.shape),
        spectral_grad[None],
    )


def solution(mesh):
    field = P(None, None, "gz", "xy", None)
    modes = P("xy", "gz", None, None, None)
    return jax.shard_map(
        body,
        mesh=mesh,
        in_specs=(field, field, modes, P(), P()),
        out_specs=(field, field, modes),
        check_vma=False,
    )
```

```python
import functools
import math

import jax
import jax.numpy as jnp
import ml_dtypes
import numpy as np
from jax import lax
from jax.experimental import pallas as pl
from jax.experimental.pallas import tpu as pltpu
from jax.sharding import PartitionSpec as P

C = 64
NX = 128
NY = 128
NZ = 128
MX = 32
MY = 32
MZ = 32
BATCH = 2
GZ = 8
XY = 32
BC = BATCH * C
ZL = NZ // GZ
XL = NX // XY
ZP = 2
PAIRS = ZL // ZP
SUB = 2 * XL
ROWS = ZP * SUB
BF = jnp.bfloat16
F32 = jnp.float32
FORWARD = (NX * NY * NZ) ** (-0.5)
INVERSE = 0.5 * (MX * MY * MZ) ** (-0.5)


def rounded(values):
    return values.astype(np.float32).astype(ml_dtypes.bfloat16).astype(np.float32)


def cos_sin(length, modes, folded):
    freq = np.arange(modes)
    if folded:
        freq = np.where(freq < modes // 2, freq, length - modes + freq)
    phase = (np.arange(length)[:, None] * freq[None, :]) % length
    angle = phase.astype(np.float32) * np.float32(2.0 * math.pi / length)
    return rounded(np.cos(angle)), rounded(np.sin(angle))


@functools.lru_cache(maxsize=None)
def tables():
    cy, sy = cos_sin(NY, MY, False)
    cx, sx = cos_sin(NX, MX, True)
    cz, sz = cos_sin(NZ, MZ, True)
    same = np.eye(XL, dtype=np.float32)
    part = np.stack([cy, -sy])
    unit = np.einsum("ryk,xv->krxvy", part, same).reshape(MY * SUB, XL * NY)
    scale = np.where(np.arange(MY) == 0, 1.0, 2.0).astype(np.float32)
    doubled = unit * np.repeat(scale, SUB)[:, None]
    z2 = np.eye(ZP, dtype=np.float32)
    fx = np.stack([np.stack([cx, sx]), np.stack([-sx, cx])])
    fx = fx.reshape(2, 2, XY, XL, MX)
    x_fwd = np.einsum("sopvk,zw->kszpwov", fx, z2).reshape(MX * 2 * ZP, XY * ROWS)
    gx = np.stack([np.stack([cx, -sx]), np.stack([sx, cx])])
    gx = gx.reshape(2, 2, XY, XL, MX)
    x_inv = np.einsum("sopvk,zw->pzsvkow", gx, z2).reshape(XY * ROWS, MX * 2 * ZP)
    kx = MX // GZ
    kxe = np.eye(kx, dtype=np.float32)
    fz = np.stack([np.stack([cz, sz]), np.stack([-sz, cz])])
    fz = fz.reshape(2, 2, GZ, PAIRS, ZP, MZ)
    z_fwd = np.einsum("sogjzm,kl->skmgjloz", fz, kxe).reshape(2 * kx * MZ, GZ * PAIRS * kx * 2 * ZP)
    gz = np.stack([np.stack([cz, -sz]), np.stack([sz, cz])])
    gz = gz.reshape(2, 2, GZ, PAIRS, ZP, MZ)
    z_inv = np.einsum("sogjzm,kl->gjkszolm", gz, kxe).reshape(GZ * PAIRS * kx * 2 * ZP, 2 * kx * MZ)
    made = dict(
        unit=unit,
        doubled=doubled,
        doubled_t=doubled.T,
        x_fwd=x_fwd,
        x_inv=x_inv,
        z_fwd=z_fwd,
        z_inv=z_inv,
    )
    return {k: np.ascontiguousarray(v).astype(ml_dtypes.bfloat16) for k, v in made.items()}


def dot(a, b, dims=((1,), (0,))):
    return lax.dot_general(a, b, (dims, ((), ())), preferred_element_type=F32)


VM = 24 * 1024 * 1024
STEPS = PAIRS // 2
CELLS = ZP * XL
STEP_CELLS = 2 * CELLS
PLANE = XL * NY
VMEM = pl.BlockSpec(memory_space=pltpu.VMEM)
REMOTE = pl.BlockSpec(memory_space=pltpu.HBM)


def far(x):
    return pltpu.with_memory_space_constraint(x, pltpu.HBM)


def call(kernel, outs, in_specs, out_specs, scratch, name, flops, nbytes):
    return pl.pallas_call(
        kernel,
        out_shape=outs,
        in_specs=in_specs,
        out_specs=out_specs,
        scratch_shapes=scratch,
        name=name,
        compiler_params=pltpu.CompilerParams(vmem_limit_bytes=VM),
        cost_estimate=pl.CostEstimate(flops=flops, bytes_accessed=nbytes, transcendentals=0),
    )


def split_pair(block):
    wide = block.astype(F32)
    n = wide.shape[0]
    halves = [wide[:, z * SUB : (z + 1) * SUB, :].reshape(n * SUB, BC) for z in range(ZP)]
    return jnp.concatenate(halves, axis=1).astype(BF)


def join_pair(wide):
    n = wide.shape[0] // SUB
    halves = [wide[:, z * BC : (z + 1) * BC].reshape(n, SUB, BC) for z in range(ZP)]
    return jnp.concatenate(halves, axis=1).astype(BF)


def chunk_of(ref, step):
    return ref.at[:, step * STEP_CELLS : (step + 1) * STEP_CELLS, :]


def aligned(index, size):
    if isinstance(index, int):
        return index * size
    return pl.multiple_of(index * size, size)


def rows_of(ref, step):
    return ref.at[step * STEP_CELLS * NY : (step + 1) * STEP_CELLS * NY, :]


def first_kernel(x_ref, far_ref, out_ref, in_ref, table_ref, wide_ref, sem):
    cells = [pl.ds(0, STEP_CELLS), pl.ds(STEP_CELLS, ZL * XL - STEP_CELLS)]
    copies = [
        pltpu.make_async_copy(x_ref.at[:, part, :], in_ref.at[:, part, :], sem.at[k])
        for k, part in enumerate(cells)
    ]
    fetch = pltpu.make_async_copy(far_ref, table_ref, sem.at[2])
    copies[0].start()
    fetch.start()
    copies[1].start()
    for i in range(STEPS):
        if i < 2:
            copies[i].wait()
        if i == 0:
            fetch.wait()
        wide_ref[i % 2] = in_ref[:, i * STEP_CELLS : (i + 1) * STEP_CELLS, :].astype(F32).reshape(BC * STEP_CELLS, NY)
        for j in range(2):
            planes = []
            for z in range(ZP):
                cells = [
                    wide_ref[i % 2, pl.ds(j * CELLS + z * XL + t, BC, stride=STEP_CELLS), :].astype(BF)
                    for t in range(XL)
                ]
                planes.append(jnp.concatenate(cells, axis=1))
            both = jnp.concatenate(planes, axis=0)
            modes = dot(table_ref[...], both, ((1,), (1,)))
            at = (2 * i + j) * ROWS
            out_ref[:, at : at + ROWS, :] = join_pair(modes)


def y_first(x, table):
    return call(
        first_kernel,
        jax.ShapeDtypeStruct((MY, PAIRS * ROWS, BC), BF),
        [REMOTE, REMOTE],
        VMEM,
        [
            pltpu.VMEM((BC, ZL * XL, NY), BF),
            pltpu.VMEM(table.shape, BF),
            pltpu.VMEM((2, BC * STEP_CELLS, NY), F32),
            pltpu.SemaphoreType.DMA((3,)),
        ],
        "y_first",
        1 << 29,
        4 << 20,
    )(far(x), far(table))


def to_lanes_kernel(x_ref, out_ref, in_ref, made_ref, wide_ref, sem, out_sem):
    copies = [
        pltpu.make_async_copy(chunk_of(x_ref, i), in_ref.at[i], sem.at[i]) for i in range(STEPS)
    ]
    for copy in copies:
        copy.start()
    outs = []
    for i in range(STEPS):
        copies[i].wait()
        wide_ref[i % 2] = in_ref[i].astype(F32).reshape(BC * STEP_CELLS, NY)
        for t in range(STEP_CELLS):
            cell = wide_ref[i % 2, pl.ds(t, BC, stride=STEP_CELLS), :]
            made_ref[i, t * NY : (t + 1) * NY, :] = cell.T.astype(BF)
        outs.append(pltpu.make_async_copy(made_ref.at[i], rows_of(out_ref, i), out_sem.at[i]))
        outs[i].start()
    for copy in outs:
        copy.wait()


def to_lanes(x):
    return call(
        to_lanes_kernel,
        jax.ShapeDtypeStruct((ZL * XL * NY, BC), BF),
        [REMOTE],
        REMOTE,
        [
            pltpu.VMEM((STEPS, BC, STEP_CELLS, NY), BF),
            pltpu.VMEM((STEPS, STEP_CELLS * NY, BC), BF),
            pltpu.VMEM((2, BC * STEP_CELLS, NY), F32),
            pltpu.SemaphoreType.DMA((STEPS,)),
            pltpu.SemaphoreType.DMA((STEPS,)),
        ],
        "to_lanes",
        0,
        12 << 20,
    )(far(x))


def from_lanes_kernel(x_ref, out_ref, in_ref, made_ref, wide_ref, in_sem, sem):
    fetches = [
        pltpu.make_async_copy(rows_of(x_ref, i), in_ref.at[i], in_sem.at[i]) for i in range(STEPS)
    ]
    for copy in fetches:
        copy.start()
    copies = []
    for i in range(STEPS):
        fetches[i].wait()
        for t in range(STEP_CELLS):
            cell = in_ref[i, t * NY : (t + 1) * NY, :].astype(F32)
            wide_ref[i % 2, pl.ds(t, BC, stride=STEP_CELLS), :] = cell.T
        made_ref[i] = wide_ref[i % 2].reshape(BC, STEP_CELLS, NY).astype(BF)
        copies.append(pltpu.make_async_copy(made_ref.at[i], chunk_of(out_ref, i), sem.at[i]))
        copies[i].start()
    for copy in copies:
        copy.wait()


def from_lanes(x):
    return call(
        from_lanes_kernel,
        jax.ShapeDtypeStruct((BC, ZL * XL, NY), BF),
        [REMOTE],
        REMOTE,
        [
            pltpu.VMEM((STEPS, STEP_CELLS * NY, BC), BF),
            pltpu.VMEM((STEPS, BC, STEP_CELLS, NY), BF),
            pltpu.VMEM((2, BC * STEP_CELLS, NY), F32),
            pltpu.SemaphoreType.DMA((STEPS,)),
            pltpu.SemaphoreType.DMA((STEPS,)),
        ],
        "from_lanes",
        0,
        12 << 20,
    )(far(x))


def x_kernel(groups_in, groups_out, scale, recv_ref, table_ref, out_ref, made_ref=None, sem=None):
    target = out_ref if made_ref is None else made_ref
    copies = []
    for i in range(STEPS):
        wide = jnp.concatenate(
            [
                recv_ref[:, (2 * i + j) * ROWS : (2 * i + j + 1) * ROWS, :].reshape(
                    groups_in * ROWS, BC
                )
                for j in range(2)
            ],
            axis=1,
        )
        done = (dot(table_ref[...], wide) * scale).astype(BF)
        for j in range(2):
            at = (2 * i + j) * ROWS
            target[:, at : at + ROWS, :] = done[:, j * BC : (j + 1) * BC].reshape(
                groups_out, ROWS, BC
            )
        if made_ref is not None and i % 2 == 1:
            rows = pl.ds((i - 1) * 2 * ROWS, 4 * ROWS)
            copies.append(
                pltpu.make_async_copy(made_ref.at[:, rows, :], out_ref.at[:, rows, :], sem.at[i // 2])
            )
            copies[-1].start()
    for copy in copies:
        copy.wait()


def x_transform(recv, table, groups_out, scale, name, away=False):
    shape = (groups_out, PAIRS * ROWS, BC)
    return call(
        functools.partial(x_kernel, recv.shape[0], groups_out, scale),
        jax.ShapeDtypeStruct(shape, BF),
        [VMEM, VMEM],
        REMOTE if away else VMEM,
        [pltpu.VMEM(shape, BF), pltpu.SemaphoreType.DMA((STEPS // 2,))] if away else [],
        name,
        1 << 27,
        2 << 20,
    )(recv, table)


GROUPS = ((0, 1), (1, 3), (3, PAIRS))


def middle_kernel(
    recv_ref,
    x_far,
    cot_far,
    inv_far,
    fwd_far,
    mix_ref,
    bias_ref,
    send_ref,
    layer_ref,
    pre_ref,
    x_ref,
    cot_ref,
    inv_ref,
    fwd_ref,
    cat_ref,
    x_sem,
    cot_sem,
    table_sem,
):
    depth = ZP * PLANE

    def moves(group):
        low, high = GROUPS[group]
        rows = pl.ds(low * depth, (high - low) * depth)
        return [
            pltpu.make_async_copy(source.at[rows, :], target.at[rows, :], sem.at[group])
            for source, target, sem in ((x_far, x_ref, x_sem), (cot_far, cot_ref, cot_sem))
        ]

    tables = [
        pltpu.make_async_copy(inv_far, inv_ref, table_sem.at[0]),
        pltpu.make_async_copy(fwd_far, fwd_ref, table_sem.at[1]),
    ]

    tables[0].start()
    for group in range(2):
        for move in moves(group):
            move.start()
        if group == 0:
            tables[1].start()

    def forward(pair):
        modes = dot(fwd_ref[...], cat_ref[pair & 1])
        send_ref[:, pl.ds(aligned(pair, ROWS), ROWS), :] = join_pair(modes)

    mix = mix_ref[...]
    none = jnp.zeros_like(mix)
    lower = jnp.concatenate(
        [jnp.concatenate([mix, none], axis=1), jnp.concatenate([none, mix], axis=1)], axis=0
    )
    bias = bias_ref[...]

    tables[0].wait()

    def step(pair, first=False):
        if not first:
            forward(pair - 1)
        block = recv_ref[:, pl.ds(aligned(pair, ROWS), ROWS), :]
        right = jnp.concatenate([split_pair(block), lower], axis=0)
        base = aligned(pair, depth)
        for t in range(XL):
            cells = [pl.ds(base + z * PLANE + t * NY, NY) for z in range(ZP)]
            left = jnp.concatenate(
                [inv_ref[t * NY : (t + 1) * NY, :]] + [x_ref[rows, :] for rows in cells], axis=1
            )
            total = dot(left, right)
            for z, rows in enumerate(cells):
                p = total[:, z * BC : (z + 1) * BC] + bias
                square = p * p
                inner = 0.7978845608 + (0.7978845608 * 0.044715) * square
                half = 0.5 + 0.5 * jnp.tanh(p * inner)
                layer_ref[rows, :] = (p * half).astype(BF)
                tail = (2.0 * 0.7978845608) + (6.0 * 0.7978845608 * 0.044715) * square
                slope = half + half * (1.0 - half) * (p * tail)
                grad = (cot_ref[rows, :].astype(F32) * slope).astype(BF)
                pre_ref[rows, :] = grad
                cat_ref[pair & 1, t * NY : (t + 1) * NY, z * BC : (z + 1) * BC] = grad

    def steps(pair, carry):
        step(pair)
        return carry

    for group, (low, high) in enumerate(GROUPS):
        for move in moves(group):
            move.wait()
        if group + 2 < len(GROUPS):
            for move in moves(group + 2):
                move.start()
        if low == 0:
            step(0, first=True)
            tables[1].wait()
            low = 1
        if high - low > 1:
            lax.fori_loop(low, high - (high - low) % 2, steps, 0, unroll=2)
        if (high - low) % 2:
            step(high - 1)
    forward(PAIRS - 1)


def middle(recv, x, cot, inv, fwd, mix, bias):
    cells = (ZL * XL * NY, BC)
    flat = jax.ShapeDtypeStruct(cells, BF)
    return call(
        middle_kernel,
        [jax.ShapeDtypeStruct((MY, PAIRS * ROWS, BC), BF), flat, flat],
        [VMEM] + [REMOTE] * 4 + [VMEM] * 2,
        [VMEM] * 3,
        [
            pltpu.VMEM(cells, BF),
            pltpu.VMEM(cells, BF),
            pltpu.VMEM(inv.shape, BF),
            pltpu.VMEM(fwd.shape, BF),
            pltpu.VMEM((2, PLANE, ZP * BC), BF),
            pltpu.SemaphoreType.DMA((len(GROUPS),)),
            pltpu.SemaphoreType.DMA((len(GROUPS),)),
            pltpu.SemaphoreType.DMA((2,)),
        ],
        "middle",
        2 << 29,
        12 << 20,
    )(recv, far(x), far(cot), far(inv), far(fwd), mix, bias)


def halves(source, target, sem):
    cut = STEP_CELLS * NY
    parts = [pl.ds(0, cut), pl.ds(cut, ZL * XL * NY - cut)]
    return [
        pltpu.make_async_copy(source.at[rows, :], target.at[rows, :], sem.at[k])
        for k, rows in enumerate(parts)
    ]


def last_kernel(recv_ref, pre_ref, inv_ref, mix_ref, out_ref, in_ref, made_ref, wide_ref, in_sem, sem):
    fetches = halves(pre_ref, in_ref, in_sem)
    for copy in fetches:
        copy.start()
    copies = []
    for i in range(STEPS):
        for j in range(2):
            pair = 2 * i + j
            modes = split_pair(recv_ref[:, pair * ROWS : (pair + 1) * ROWS, :])
            cells = dot(modes, inv_ref[...], ((0,), (0,)))
            if j == 0 and i < len(fetches):
                fetches[i].wait()
            at = pair * ZP * PLANE
            rows = in_ref[at : at + ZP * PLANE, :]
            local = dot(mix_ref[...], rows, ((1,), (1,)))
            for z in range(ZP):
                for t in range(XL):
                    at = z * XL + t
                    wide_ref[i % 2, pl.ds(j * CELLS + at, BC, stride=STEP_CELLS), :] = (
                        cells[z * BC : (z + 1) * BC, t * NY : (t + 1) * NY]
                        + local[:, at * NY : (at + 1) * NY]
                    )
        made_ref[i] = wide_ref[i % 2].reshape(BC, STEP_CELLS, NY).astype(BF)
        copies.append(pltpu.make_async_copy(made_ref.at[i], chunk_of(out_ref, i), sem.at[i]))
        copies[i].start()
    for copy in copies:
        copy.wait()


def last(recv, pre, inv, mix):
    return call(
        last_kernel,
        jax.ShapeDtypeStruct((BC, ZL * XL, NY), BF),
        [VMEM, REMOTE, VMEM, VMEM],
        REMOTE,
        [
            pltpu.VMEM((ZL * XL * NY, BC), BF),
            pltpu.VMEM((STEPS, BC, STEP_CELLS, NY), BF),
            pltpu.VMEM((2, BC * STEP_CELLS, NY), F32),
            pltpu.SemaphoreType.DMA((2,)),
            pltpu.SemaphoreType.DMA((STEPS,)),
        ],
        "last",
        2 << 29,
        8 << 20,
    )(recv, far(pre), inv, mix)


def exchange(x, axis):
    return lax.all_to_all(x, axis, split_axis=0, concat_axis=0, tiled=True)


KX = MX // GZ


def z_forward_kernel(recv_ref, table_ref, real_ref, imag_ref):
    half = KX * MZ
    rows = recv_ref[...].reshape(GZ * PAIRS * ROWS, BC)
    real_ref[...] = dot(table_ref[:half, :], rows).astype(BF)
    imag_ref[...] = dot(table_ref[half:, :], rows).astype(BF)


def z_forward(recv, table):
    part = jax.ShapeDtypeStruct((KX * MZ, BC), BF)
    parts = call(
        z_forward_kernel,
        [part, part],
        [VMEM] * 2,
        [VMEM] * 2,
        [],
        "z_forward",
        1 << 26,
        1 << 20,
    )(recv, table)
    return [x.reshape(KX, MZ, BATCH, C) for x in parts]


def z_inverse_kernel(real_ref, imag_ref, table_ref, out_ref):
    half = KX * MZ
    total = dot(table_ref[:, :half], real_ref[...]) + dot(table_ref[:, half:], imag_ref[...])
    out_ref[...] = total.astype(BF).reshape(GZ, PAIRS * ROWS, BC)


def z_inverse(real, imag, table):
    return call(
        z_inverse_kernel,
        jax.ShapeDtypeStruct((GZ, PAIRS * ROWS, BC), BF),
        [VMEM] * 3,
        VMEM,
        [],
        "z_inverse",
        1 << 26,
        1 << 20,
    )(real.reshape(KX * MZ, BC), imag.reshape(KX * MZ, BC), table)


def body(features, cotangent, spectral, pointwise, channel_bias):
    t = {k: jnp.asarray(v) for k, v in tables().items()}
    x = features.reshape(BC, ZL * XL, NY)
    cot = cotangent.reshape(BC, ZL * XL, NY)
    weights = spectral[0]
    mix = jnp.zeros((BATCH, C, BATCH, C), BF)
    mix = mix.at[0, :, 0, :].set(pointwise).at[1, :, 1, :].set(pointwise).reshape(BC, BC)
    bias = jnp.tile(channel_bias, BATCH)[None, :]

    recv = exchange(y_first(x, t["unit"]), "xy")
    x_lanes = to_lanes(x)
    recv = exchange(x_transform(recv, t["x_fwd"], GZ, FORWARD, "x_forward"), "gz")
    spectra = jnp.stack(z_forward(recv, t["z_fwd"]))
    products = jnp.einsum("rkmbi,kmio->rkmbo", spectra, weights, preferred_element_type=F32)
    real = (products[0, ..., :C] - products[1, ..., C:]).astype(BF)
    imag = (products[0, ..., C:] + products[1, ..., :C]).astype(BF)
    recv = exchange(z_inverse(real, imag, t["z_inv"]), "gz")
    recv = exchange(x_transform(recv, t["x_inv"], XY, INVERSE, "x_inverse", True), "xy")
    cot_lanes = to_lanes(cot)
    send, layer, pre = middle(
        recv, x_lanes, cot_lanes, t["doubled_t"], t["doubled"], mix, bias
    )
    recv = exchange(send, "xy")
    layer_out = from_lanes(layer)
    recv = exchange(x_transform(recv, t["x_fwd"], GZ, INVERSE, "x_forward"), "gz")
    real, imag = z_forward(recv, t["z_fwd"])
    paired = jnp.stack(
        [
            jnp.concatenate([real, imag], axis=-1),
            jnp.concatenate([imag, -real], axis=-1),
        ]
    )
    spectra_grad = jnp.einsum(
        "rkmbo,kmio->rkmbi", paired, weights, preferred_element_type=F32
    ).astype(BF)
    recv = exchange(z_inverse(spectra_grad[0], spectra_grad[1], t["z_inv"]), "gz")
    recv = exchange(x_transform(recv, t["x_inv"], XY, FORWARD, "x_inverse", True), "xy")
    spectral_grad = jnp.einsum(
        "rkmbi,rkmbo->kmio", spectra, paired, preferred_element_type=F32
    ).astype(BF)
    input_grad = last(recv, pre, t["unit"], mix)
    return (
        layer_out.reshape(features.shape),
        input_grad.reshape(features.shape),
        spectral_grad[None],
    )


def solution(mesh):
    field = P(None, None, "gz", "xy", None)
    modes = P("xy", "gz", None, None, None)
    return jax.shard_map(
        body,
        mesh=mesh,
        in_specs=(field, field, modes, P(), P()),
        out_specs=(field, field, modes),
        check_vma=False,
    )
```
